32 devices in a mesh: section: 16 (over z, y, x), attn: 2 (over core).
Axes of the slice: x: 2, y: 2, z: 4, core: 2. Of those that a mesh axis runs over, the one named last changes fastest.
Arguments:
- queries: bfloat16 [8192, 3072], P(('section', 'attn')), may hold values from -120 to 120
- keys: bfloat16 [8192, 1024], P(('section', 'attn')), may hold values from -2.5 to 2.5
- values: bfloat16 [8192, 1024], P(('section', 'attn')), may hold values from -4 to 4
- doc_ids: int32 [8192], replicated, may hold values from 0 to 15, never falling along the last dimension, each value on 1 to 1792 neighbouring positions
Outputs:
- attended: bfloat16 [8192, 3072], P(('section', 'attn'))
The draws below stay inside these ranges and needn't reach their ends.
Inputs may be any that keep to these rules, and one draw needn't show every extreme that they name: `doc_ids`: along the pack the document numbers never fall, and a document holds at most 1792 tokens.
All inputs are finite; a program needn't handle non-finite values.
Results may differ from the reference program's by a relative error of at most 0.0028.
Values may be sent and summed in bfloat16 or wider, within the bound.
No kernel may reach another device: no remote copies, remote signals or barrier semaphores. Data moves between devices by JAX's collectives and lax.ppermute only.
A program may use at most 64 MiB of HBM per device.

```python
import math
import jax
import jax.numpy as jnp
import numpy as np
from jax import lax

D = 3072
KV_HEADS = 8
HEAD_DIM = 128
TOK_DEV = 256
GROUP = 3
REACH = 8
TOKENS = 8192
DOC_MOST = 1792
DOCS = 16
DEVICES = 32


def shared_fields(key):
    base = jax.random.fold_in(key, 4242)
    pairs = TOKENS // 2
    key_base = jnp.clip(jax.random.normal(jax.random.fold_in(base, 1), (pairs, 2, KV_HEADS, HEAD_DIM), jnp.float32), -2.5, 2.5)
    query_base = jnp.clip(2.5 * jax.random.normal(jax.random.fold_in(base, 2), (pairs, 2, KV_HEADS, GROUP, HEAD_DIM), jnp.float32), -7.5, 7.5)
    return (key_base, query_base)


def draw_queries(key, part):
    key_base, query_base = shared_fields(key)
    chosen = query_base
    return chosen.reshape(TOKENS, KV_HEADS * GROUP * HEAD_DIM).astype(jnp.bfloat16)


def draw_keys(key, part):
    key_base, query_base = shared_fields(key)
    chosen = key_base
    return chosen.reshape(TOKENS, KV_HEADS * HEAD_DIM).astype(jnp.bfloat16)


def block_levels(key, dims, pieces, low, top_value):
    factor_of, own = 1.0, jax.random.fold_in(key, 6)
    for axis_at, shards_of in pieces:
        heights = jnp.exp(jax.random.uniform(jax.random.fold_in(own, axis_at), (shards_of,), jnp.float32, low / len(pieces), top_value / len(pieces)))
        factor_of = factor_of * jnp.repeat(heights, dims[axis_at] // shards_of).reshape([-1 if axis == axis_at else 1 for axis in range(len(dims))])
    return factor_of


def profile(number_of, total, bound, lean):
    portions = [(1 << 20) // math.isqrt(standing ** lean) + 1 for standing in range(2, number_of + 1)]
    surplus, counts = total - bound - (number_of - 1), [1] * (number_of - 1)
    while surplus > 0:
        free = [i for i in range(number_of - 1) if counts[i] < bound]
        pool, left = sum([portions[i] for i in free]), surplus
        for i in free:
            more = min(bound - counts[i], max(1, left * portions[i] // pool), surplus)
            counts[i] = counts[i] + more
            surplus = surplus - more
    return np.array([bound] + counts)


def uneven(stream_key, count, total, bound, slope):
    if count == 2:
        one = jax.random.randint(stream_key, (), max(1, total - bound), min(bound, total - 1) + 1)
        return jnp.stack([one, total - one])
    lengths = jnp.asarray(profile(count, total, bound, slope), jnp.int32)
    twos = (count - 1) // 2
    giver, sink = lengths[1:1 + 2 * twos:2], lengths[2:2 + 2 * twos:2]
    room = jnp.minimum(giver - 1, bound - sink)
    passed = jax.random.randint(jax.random.fold_in(stream_key, 1), (twos,), 0, 1 << 20) % (room + 1)
    lengths = lengths.at[1:1 + 2 * twos:2].set(giver - passed).at[2:2 + 2 * twos:2].set(sink + passed)
    return lengths[jax.random.permutation(jax.random.fold_in(stream_key, 2), count)]


def centred(key, extent, spread, reach, split=(), held_as=jnp.bfloat16):
    array = spread * jax.random.normal(key, extent, jnp.float32)
    if split:
        array = array * block_levels(key, extent, split, -0.22, 0.18)
    return jnp.clip(array, -reach, reach).astype(held_as)


def setup_inputs(seed: int = 0) -> dict:
    seeds = jax.random.split(jax.random.key(seed), 5)
    queries = draw_queries(jax.random.fold_in(seeds[4], 71), 0)
    keys = draw_keys(jax.random.fold_in(seeds[4], 71), 0)
    values = centred(seeds[2], (TOKENS, KV_HEADS * HEAD_DIM), 1.0, 4.0, ((0, 32),))
    doc_ids = jnp.searchsorted(jnp.cumsum(uneven(seeds[3], DOCS, TOKENS, DOC_MOST, 2)), jnp.arange(TOKENS), side="right").astype(jnp.int32)
    return {"queries": queries, "keys": keys, "values": values, "doc_ids": doc_ids}


def reference(queries, keys, values, doc_ids):
    span = REACH * TOK_DEV
    lead = span - TOK_DEV
    width = KV_HEADS * HEAD_DIM
    query_blocks = queries.reshape(DEVICES, TOK_DEV, KV_HEADS, GROUP, HEAD_DIM)
    padded_keys = jnp.concatenate([jnp.zeros((lead, width), keys.dtype), keys], axis=0).reshape(-1, KV_HEADS, HEAD_DIM)
    padded_values = jnp.concatenate([jnp.zeros((lead, width), values.dtype), values], axis=0).reshape(-1, KV_HEADS, HEAD_DIM)
    all_ids = doc_ids.astype(jnp.int32)
    padded_ids = jnp.concatenate([jnp.full((lead,), -1, jnp.int32), all_ids], axis=0)
    local_rows = jnp.arange(TOK_DEV, dtype=jnp.int32)
    window_rows = jnp.arange(span, dtype=jnp.int32)

    def one_block(operands):
        block_queries, block_index = operands
        first = block_index * TOK_DEV
        window_keys = lax.dynamic_slice_in_dim(padded_keys, first, span, 0)
        window_values = lax.dynamic_slice_in_dim(padded_values, first, span, 0)
        window_ids = lax.dynamic_slice_in_dim(padded_ids, first, span, 0)
        query_ids = lax.dynamic_slice_in_dim(all_ids, first, TOK_DEV, 0)
        query_pos = first + local_rows
        key_pos = first - lead + window_rows
        allowed = (key_pos[None, :] <= query_pos[:, None]) & (window_ids[None, :] == query_ids[:, None])
        scores = jnp.einsum("qgrd,kgd->grqk", block_queries.astype(jnp.float32), window_keys.astype(jnp.float32), precision=lax.Precision.HIGHEST) * (HEAD_DIM ** -0.5)
        scores = jnp.where(allowed[None, None], scores, -1e30)
        weights = jnp.exp(scores - jnp.max(scores, axis=-1, keepdims=True))
        total = jnp.sum(weights, axis=-1)
        rounded = lax.optimization_barrier(weights.astype(jnp.bfloat16)).astype(jnp.float32)
        weighted = jnp.einsum("grqk,kgd->grqd", rounded, window_values.astype(jnp.float32), precision=lax.Precision.HIGHEST)
        return (weighted / total[..., None]).astype(jnp.bfloat16).transpose(2, 0, 1, 3)

    attended = lax.map(one_block, (query_blocks, jnp.arange(DEVICES, dtype=jnp.int32)))
    return attended.reshape(TOKENS, D)
```

```python
import functools
import math

import jax
import jax.numpy as jnp
from jax import lax
from jax.experimental import pallas as pl
from jax.experimental.pallas import tpu as pltpu
from jax.sharding import PartitionSpec as P

HEAD_DIM = 128
REACH = 8
AXES = ("section", "attn")
NEG = -1e30
SCALE = HEAD_DIM ** -0.5 * math.log2(math.e)
HEADS_STEP = 2
barrier = lax.optimization_barrier


def fold(q, carry, k, v, allowed):
    s = lax.dot_general(q, k, (((1,), (1,)), ((), ())), preferred_element_type=jnp.float32)
    s = jnp.where(allowed, s, NEG)
    top = jnp.max(s, axis=1, keepdims=True)
    if carry is not None:
        top = jnp.maximum(top, carry[0])
    w = jnp.exp2((s - top) * SCALE)
    total = jnp.sum(w, axis=1, keepdims=True)
    out = jnp.dot(w.astype(jnp.bfloat16), v, preferred_element_type=jnp.float32)
    if carry is not None:
        back = jnp.exp2((carry[0] - top) * SCALE)
        total = total + carry[1] * back
        out = out + carry[2] * back
    return top, total, out


def read_stats(ref, h, g):
    at = h * HEAD_DIM + 2 * g
    return ref[:, at:at + 1], ref[:, at + 1:at + 2]


def write_stats(ref, h, pairs):
    rows = ref.shape[0]
    lane = lax.broadcasted_iota(jnp.int32, (rows, HEAD_DIM), 1)
    tile = jnp.zeros((rows, HEAD_DIM), jnp.float32)
    for g, (top, total) in enumerate(pairs):
        tile = jnp.where(lane == 2 * g, top, jnp.where(lane == 2 * g + 1, total, tile))
    ref[:, h * HEAD_DIM:(h + 1) * HEAD_DIM] = tile


def cut(ref, h, width=HEAD_DIM):
    return ref[:, h * width:(h + 1) * width]


def own_kernel(group, info, q_ref, start_ref, k_ref, v_ref, mk_ref, mv_ref, acc_ref, stat_ref):
    rows = q_ref.shape[0]
    start = start_ref[...]
    at = lax.broadcasted_iota(jnp.int32, (rows, rows), 1)
    row = lax.broadcasted_iota(jnp.int32, (rows, rows), 0)
    own_ok = (at <= row) & (at + info[0] >= start)
    mate_ok = at + info[1] >= start
    allowed = jnp.concatenate([own_ok, mate_ok], axis=1)
    for h in range(HEADS_STEP):
        k = jnp.concatenate([cut(k_ref, h), cut(mk_ref, h)], axis=0)
        v = jnp.concatenate([cut(v_ref, h), cut(mv_ref, h)], axis=0)
        pairs = []
        for g in range(group):
            head = h * group + g
            top, total, out = fold(cut(q_ref, head), None, k, v, allowed)
            acc_ref[:, head * HEAD_DIM:(head + 1) * HEAD_DIM] = out
            pairs.append((top, total))
        write_stats(stat_ref, h, pairs)


def far_kernel(group, choose, last, info, q_ref, start_ref, acc_in, stat_in, *refs):
    rows = q_ref.shape[0]
    pieces, outs = (refs[:-1], refs[-1:]) if last else (refs[:-2], refs[-2:])
    needed = info[1] > 0

    def done(head, total, out):
        outs[0][:, head * HEAD_DIM:(head + 1) * HEAD_DIM] = (out / total).astype(jnp.bfloat16)

    @pl.when(needed)
    def _():
        start = start_ref[...]
        at = lax.broadcasted_iota(jnp.int32, (rows, rows), 1)
        allowed = jnp.concatenate([at + info[2 + i] >= start for i in range(4)], axis=1)
        for h in range(HEADS_STEP):
            ks, vs = choose(info[0], [cut(r, h) for r in pieces])
            k, v = jnp.concatenate(ks, axis=0), jnp.concatenate(vs, axis=0)
            pairs = []
            for g in range(group):
                head = h * group + g
                carry = read_stats(stat_in, h, g) + (cut(acc_in, head),)
                top, total, out = fold(cut(q_ref, head), carry, k, v, allowed)
                if last:
                    done(head, total, out)
                else:
                    outs[0][:, head * HEAD_DIM:(head + 1) * HEAD_DIM] = out
                    pairs.append((top, total))
            if not last:
                write_stats(outs[1], h, pairs)

    @pl.when(jnp.logical_not(needed))
    def _():
        if last:
            for h in range(HEADS_STEP):
                for g in range(group):
                    done(h * group + g, read_stats(stat_in, h, g)[1], cut(acc_in, h * group + g))
        else:
            outs[0][...] = acc_in[...]
            outs[1][...] = stat_in[...]


def pick(plane, at0, at1, at2, at3):
    return jnp.where(plane == 0, at0, jnp.where(plane == 1, at1, jnp.where(plane == 2, at2, at3)))


def choose_middle(plane, tiles):
    def half(x1, y1, z1, x2, y2, z2, first_k):
        pk, pv = pick(plane, z2, x1, y1, x1), pick(plane, x2, x2, y2, x2)
        qk, qv = pick(plane, first_k, y2, x2, y2), pick(plane, z1, z2, z2, y1)
        return pk, pv, qk, qv
    near, far = tiles[:6], tiles[6:]
    a, b = half(*near, far[2]), half(*far, far[2])
    return (a[0], b[0], a[2], b[2]), (a[1], b[1], a[3], b[3])


def choose_last(plane, tiles):
    def half(z1, y2, x3, y3, z3):
        pk, pv = pick(plane, z3, y3, y3, y3), pick(plane, y2, x3, x3, x3)
        qk, qv = pick(plane, x3, z3, z3, z1), pick(plane, y3, z1, z1, z3)
        return pk, pv, qk, qv
    a, b = half(*tiles[:5]), half(*tiles[5:])
    return (a[0], b[0], a[2], b[2]), (a[1], b[1], a[3], b[3])


def call(kernel, info, q, start, carry, pieces, last, keys):
    rows, width = q.shape
    heads = pieces[0].shape[1] // HEAD_DIM
    group = width // pieces[0].shape[1]
    step = HEADS_STEP * HEAD_DIM

    def block(columns):
        return pl.BlockSpec((rows, columns), lambda j, *_: (0, j))

    wide, narrow = block(group * step), block(step)
    out_shape = [jax.ShapeDtypeStruct(q.shape, jnp.bfloat16 if last else jnp.float32)]
    out_specs = [wide]
    if not last:
        out_shape.append(jax.ShapeDtypeStruct((rows, heads * HEAD_DIM), jnp.float32))
        out_specs.append(narrow)
    return pl.pallas_call(
        functools.partial(kernel, group),
        grid_spec=pltpu.PrefetchScalarGridSpec(
            num_scalar_prefetch=1,
            grid=(heads // HEADS_STEP,),
            in_specs=[wide, pl.BlockSpec((rows, 1), lambda j, *_: (0, 0))]
            + [wide, narrow][:len(carry)] + [narrow] * len(pieces),
            out_specs=out_specs,
        ),
        out_shape=out_shape,
        cost_estimate=pl.CostEstimate(
            flops=8 * rows * keys * width, bytes_accessed=4 * rows * width, transcendentals=0
        ),
        compiler_params=pltpu.CompilerParams(vmem_limit_bytes=40 * 2**20),
    )(info, q, start, *carry, *pieces)


def shards(queries, keys, values, doc_ids):
    rows = queries.shape[0]
    chips, cores = lax.axis_size("section"), lax.axis_size("attn")
    chip, core = lax.axis_index("section"), lax.axis_index("attn")
    owner = chip * cores + core
    plane, odd_x, odd_y = chip % 4, chip % 2, (chip // 2) % 2

    def routes(target):
        return [(c * cores + k, target(c) * cores + k) for c in range(chips) for k in range(cores)]

    along = {"x": routes(lambda c: c ^ 1), "y": routes(lambda c: c ^ 2), "z": routes(lambda c: (c + 4) % chips)}
    along["mate"] = [(c * cores + k, c * cores + 1 - k) for c in range(chips) for k in range(cores)]

    def send(array, way):
        return lax.ppermute(array, AXES, along[way])

    def round_of(x, y, z, *mates):
        x, y, z, *mates = barrier((x, y, z) + mates)
        z, x, y = send(z, "z"), send(x, "x"), send(y, "y")
        mates = [send(m, "mate") for m in mates]
        return barrier((x, y, z)) + tuple(mates)

    def swap(*arrays):
        return tuple(send(a, "mate") for a in arrays)

    first = owner * rows
    span = min(REACH * rows, doc_ids.shape[0])
    low = jnp.maximum(first - (REACH - 1) * rows, 0)
    window = lax.dynamic_slice_in_dim(doc_ids, low, span)
    query_doc = lax.dynamic_slice_in_dim(doc_ids, first, rows)
    start = low + jnp.sum((window[None, :] < query_doc[:, None]).astype(jnp.int32), axis=1, keepdims=True)
    none = jnp.int32(-(2**30))

    def place(device, ok=True):
        return jnp.where((device >= 0) & (device < owner) & ok, device * rows, none)

    def info_of(places):
        newest = functools.reduce(jnp.maximum, places)
        needed = (newest + rows > start[0, 0]).astype(jnp.int32)
        return jnp.stack([plane, needed] + places)

    def halves(back):
        base = (chip - back) * cores
        return [place(base + core), place(base + 1 - core)]

    own_info = jnp.stack([first, place(owner - 1, core == 1)])
    extra = place(chip * cores - 7, core == 0)
    q_places = halves(pick(plane, 0, 2, 3, 2))
    q_places = [jnp.where(plane == 0, extra, q_places[0]), jnp.where(plane == 0, none, q_places[1])]
    middle_info = info_of(halves(pick(plane, 3, 1, 2, 1)) + q_places)
    last_info = info_of(halves(pick(plane, 2, 3, 1, 3)) + halves(pick(plane, 1, 4, 4, 4)))

    mate_v = send(values, "mate")
    w = jnp.where
    x1, y1, z1, mate_k = round_of(
        w(plane == 3, values, keys),
        w(odd_x == 1, values, keys),
        w((plane == 1) | (plane == 2), values, w((plane == 0) & (core == 0), mate_v, keys)),
        keys,
    )
    acc, stat = call(own_kernel, own_info, queries, start, (), [keys, values, mate_k, mate_v], False, 2 * rows)
    x2, y2, z2 = round_of(
        w(odd_x == 0, values, z1),
        w(odd_y == 1, z1, w(odd_x == 0, values, keys)),
        w(plane == 1, y1, x1),
    )
    x1s, y1s, z1s = swap(x1, y1, z1)
    x3, y3, z3 = round_of(
        w(plane == 3, y1, y2),
        w(odd_y == 0, x1, z2),
        w(plane == 0, y1, w(plane == 3, values, keys)),
    )
    x2s, y2s, z2s = swap(x2, y2, z2)
    acc, stat = call(
        lambda group, *refs: far_kernel(group, choose_middle, False, *refs),
        middle_info, queries, start, (acc, stat),
        [x1, y1, z1, x2, y2, z2, x1s, y1s, z1s, x2s, y2s, z2s], False, 4 * rows,
    )
    x3s, y3s, z3s = swap(x3, y3, z3)
    (out,) = call(
        lambda group, *refs: far_kernel(group, choose_last, True, *refs),
        last_info, queries, start, (acc, stat),
        [z1, y2, x3, y3, z3, z1s, y2s, x3s, y3s, z3s], True, 4 * rows,
    )
    return out


def solution(mesh):
    split = P(AXES, None)
    return jax.shard_map(
        shards, mesh=mesh, in_specs=(split, split, split, P()), out_specs=split, check_vma=False
    )
```

```python
import functools
import math

import jax
import jax.numpy as jnp
from jax import lax
from jax.experimental import pallas as pl
from jax.experimental.pallas import tpu as pltpu
from jax.sharding import PartitionSpec as P

HEAD_DIM = 128
REACH = 8
AXES = ("section", "attn")
NEG = -1e30
SCALE = HEAD_DIM ** -0.5 * math.log2(math.e)
HEADS_STEP = 2
HIGH = 60.0
barrier = lax.optimization_barrier


def scores(q, k, allowed):
    s = lax.dot_general(q, k, (((1,), (1,)), ((), ())), preferred_element_type=jnp.float32)
    return jnp.where(allowed, s, NEG)


def weigh(w, v):
    total = jnp.sum(w, axis=1, keepdims=True)
    return total, jnp.dot(w.astype(jnp.bfloat16), v, preferred_element_type=jnp.float32)


def read_stats(ref, head):
    return ref[:, 2 * head:2 * head + 1], ref[:, 2 * head + 1:2 * head + 2]


def write_stats(ref, pairs):
    lane = lax.broadcasted_iota(jnp.int32, ref.shape, 1)
    tile = jnp.zeros(ref.shape, jnp.float32)
    for head, (top, total) in enumerate(pairs):
        tile = jnp.where(lane == 2 * head, top, jnp.where(lane == 2 * head + 1, total, tile))
    ref[...] = tile


def cut(ref, h, width=HEAD_DIM):
    return ref[:, h * width:(h + 1) * width]


def own_kernel(group, info, q_ref, start_ref, k_ref, v_ref, mk_ref, mv_ref, acc_ref, stat_ref):
    rows = q_ref.shape[0]
    start = start_ref[...]
    at = lax.broadcasted_iota(jnp.int32, (rows, rows), 1)
    row = lax.broadcasted_iota(jnp.int32, (rows, rows), 0)
    own_ok = (at <= row) & (at + info[0] >= start)
    mate_ok = at + info[1] >= start
    allowed = jnp.concatenate([own_ok, mate_ok], axis=1)
    pairs = []
    for h in range(HEADS_STEP):
        k = jnp.concatenate([cut(k_ref, h), cut(mk_ref, h)], axis=0)
        v = jnp.concatenate([cut(v_ref, h), cut(mv_ref, h)], axis=0)
        for head in range(h * group, (h + 1) * group):
            s = scores(cut(q_ref, head), k, allowed)
            top = jnp.max(s, axis=1, keepdims=True)
            total, out = weigh(jnp.exp2((s - top) * SCALE), v)
            acc_ref[:, head * HEAD_DIM:(head + 1) * HEAD_DIM] = out
            pairs.append((top, total))
    write_stats(stat_ref, pairs)


def far_kernel(group, choose, last, info, q_ref, start_ref, acc_in, stat_in, *refs):
    rows = q_ref.shape[0]
    pieces, outs = (refs[:-1], refs[-1:]) if last else (refs[:-2], refs[-2:])
    heads = HEADS_STEP * group
    needed = info[1] > 0

    def put(head, total, out):
        if last:
            out = (out / total).astype(jnp.bfloat16)
        outs[0][:, head * HEAD_DIM:(head + 1) * HEAD_DIM] = out

    def attend(exact):
        start = start_ref[...]
        at = lax.broadcasted_iota(jnp.int32, (rows, rows), 1)
        allowed = jnp.concatenate([at + info[2 + i] >= start for i in range(4)], axis=1)
        pairs, high = [], None
        for h in range(HEADS_STEP):
            ks, vs = choose(info[0], [cut(r, h) for r in pieces])
            k, v = jnp.concatenate(ks, axis=0), jnp.concatenate(vs, axis=0)
            for head in range(h * group, (h + 1) * group):
                s = scores(cut(q_ref, head), k, allowed)
                top, total = read_stats(stat_in, head)
                before = cut(acc_in, head)
                if exact:
                    new = jnp.maximum(top, jnp.max(s, axis=1, keepdims=True))
                    back = jnp.exp2((top - new) * SCALE)
                    top, total, before = new, total * back, before * back
                power = (s - top) * SCALE
                if not exact:
                    peak = jnp.max(power.reshape(rows // 8, 8, -1, HEAD_DIM), axis=(0, 2))
                    high = peak if high is None else jnp.maximum(high, peak)
                more, out = weigh(jnp.exp2(power), v)
                total = total + more
                put(head, total, out + before)
                pairs.append((top, total))
        if not last:
            write_stats(outs[1], pairs)
        return high

    @pl.when(needed)
    def _():
        high = attend(False)

        @pl.when(jnp.max(high) > HIGH)
        def _():
            attend(True)

    @pl.when(jnp.logical_not(needed))
    def _():
        for head in range(heads):
            put(head, read_stats(stat_in, head)[1], cut(acc_in, head))
        if not last:
            outs[1][...] = stat_in[...]


def pick(plane, at0, at1, at2, at3):
    return jnp.where(plane == 0, at0, jnp.where(plane == 1, at1, jnp.where(plane == 2, at2, at3)))


def choose_middle(plane, tiles):
    def half(x1, y1, z1, x2, y2, z2, odd_k, odd_v):
        pk, pv = pick(plane, x2, x2, y2, x2), pick(plane, z2, x1, y1, x1)
        qk, qv = pick(plane, odd_k, y2, x2, y2), pick(plane, odd_v, z2, z2, y1)
        return pk, pv, qk, qv
    near, far = tiles[:6], tiles[6:]
    a, b = half(*near, far[2], near[2]), half(*far, far[2], near[2])
    return (a[0], b[0], a[2], b[2]), (a[1], b[1], a[3], b[3])


def choose_last(plane, tiles):
    def half(z1, y2, x3, y3, z3):
        pk, pv = pick(plane, y2, x3, x3, x3), pick(plane, z3, y3, y3, y3)
        qk, qv = pick(plane, x3, z1, z1, z1), pick(plane, y3, z3, z3, z3)
        return pk, pv, qk, qv
    a, b = half(*tiles[:5]), half(*tiles[5:])
    return (a[0], b[0], a[2], b[2]), (a[1], b[1], a[3], b[3])


def call(kernel, info, q, start, carry, pieces, last, keys):
    rows, width = q.shape
    heads = pieces[0].shape[1] // HEAD_DIM
    group = width // pieces[0].shape[1]
    step = HEADS_STEP * HEAD_DIM

    def block(columns):
        return pl.BlockSpec((rows, columns), lambda j, *_: (0, j))

    wide, narrow, stats = block(group * step), block(step), block(HEAD_DIM)
    out_shape = [jax.ShapeDtypeStruct(q.shape, jnp.bfloat16 if last else jnp.float32)]
    out_specs = [wide]
    if not last:
        out_shape.append(jax.ShapeDtypeStruct((rows, heads // HEADS_STEP * HEAD_DIM), jnp.float32))
        out_specs.append(stats)
    return pl.pallas_call(
        functools.partial(kernel, group),
        grid_spec=pltpu.PrefetchScalarGridSpec(
            num_scalar_prefetch=1,
            grid=(heads // HEADS_STEP,),
            in_specs=[wide, pl.BlockSpec((rows, 1), lambda j, *_: (0, 0))]
            + [wide, stats][:len(carry)] + [narrow] * len(pieces),
            out_specs=out_specs,
        ),
        out_shape=out_shape,
        cost_estimate=pl.CostEstimate(
            flops=8 * rows * keys * width, bytes_accessed=4 * rows * width, transcendentals=0
        ),
        compiler_params=pltpu.CompilerParams(vmem_limit_bytes=40 * 2**20),
    )(info, q, start, *carry, *pieces)


def shards(queries, keys, values, doc_ids):
    rows = queries.shape[0]
    chips, cores = lax.axis_size("section"), lax.axis_size("attn")
    chip, core = lax.axis_index("section"), lax.axis_index("attn")
    owner = chip * cores + core
    plane, odd_x, odd_y = chip % 4, chip % 2, (chip // 2) % 2

    def routes(target):
        return [(c * cores + k, target(c) * cores + k) for c in range(chips) for k in range(cores)]

    along = {"x": routes(lambda c: c ^ 1), "y": routes(lambda c: c ^ 2), "z": routes(lambda c: (c + 4) % chips)}
    along["mate"] = [(c * cores + k, c * cores + 1 - k) for c in range(chips) for k in range(cores)]

    def send(array, way):
        return lax.ppermute(array, AXES, along[way])

    def swap(*arrays):
        return tuple(send(a, "mate") for a in arrays)

    first = owner * rows
    span = min(REACH * rows, doc_ids.shape[0])
    low = jnp.maximum(first - (REACH - 1) * rows, 0)
    window = lax.dynamic_slice_in_dim(doc_ids, low, span)
    query_doc = lax.dynamic_slice_in_dim(doc_ids, first, rows)
    start = low + jnp.sum((window[None, :] < query_doc[:, None]).astype(jnp.int32), axis=1, keepdims=True)
    none = jnp.int32(-(2**30))

    def place(device, ok=True):
        return jnp.where((device >= 0) & (device < owner) & ok, device * rows, none)

    def info_of(places):
        newest = functools.reduce(jnp.maximum, places)
        needed = (newest + rows > start[0, 0]).astype(jnp.int32)
        return jnp.stack([plane, needed] + places)

    def halves(back):
        base = (chip - back) * cores
        return [place(base + core), place(base + 1 - core)]

    own_info = jnp.stack([first, place(owner - 1, core == 1)])
    extra = place(chip * cores - 7, core == 0)
    q_places = halves(pick(plane, 0, 2, 3, 2))
    q_places = [jnp.where(plane == 0, extra, q_places[0]), jnp.where(plane == 0, none, q_places[1])]
    middle_info = info_of(halves(pick(plane, 3, 1, 2, 1)) + q_places)
    last_info = info_of(halves(pick(plane, 2, 3, 1, 3)) + halves(pick(plane, 1, 4, 4, 4)))

    w = jnp.where
    mate_k, mate_v = swap(keys, values)
    x1, y1 = send(values, "x"), send(values, "y")
    z1 = send(w((plane == 0) & (core == 0), mate_v, keys), "z")
    acc, stat = call(own_kernel, own_info, queries, start, (), [keys, values, mate_k, mate_v], False, 2 * rows)
    x1, y1, z1, acc, stat, middle_info, last_info = barrier((x1, y1, z1, acc, stat, middle_info, last_info))
    x2 = send(w(odd_x == 0, keys, z1), "x")
    y2 = send(w(odd_y == 0, keys, z1), "y")
    z2 = send(w(plane == 1, y1, x1), "z")
    x1s, y1s, z1s = swap(x1, y1, z1)
    x2, y2, z2 = barrier((x2, y2, z2))
    x3 = send(y2, "x")
    y3 = send(w(odd_y == 0, x1, z2), "y")
    z3 = send(w(plane == 0, y1, values), "z")
    x2s, y2s, z2s = swap(x2, y2, z2)
    acc, stat = call(
        lambda group, *refs: far_kernel(group, choose_middle, False, *refs),
        middle_info, queries, start, (acc, stat),
        [x1, y1, z1, x2, y2, z2, x1s, y1s, z1s, x2s, y2s, z2s], False, 4 * rows,
    )
    x3, y3, z3, acc, stat = barrier((x3, y3, z3, acc, stat))
    x3s, y3s, z3s = swap(x3, y3, z3)
    (out,) = call(
        lambda group, *refs: far_kernel(group, choose_last, True, *refs),
        last_info, queries, start, (acc, stat),
        [z1, y2, x3, y3, z3, z1s, y2s, x3s, y3s, z3s], True, 4 * rows,
    )
    return out


def solution(mesh):
    split = P(AXES, None)
    return jax.shard_map(
        shards, mesh=mesh, in_specs=(split, split, split, P()), out_specs=split, check_vma=False
    )
```

```python
import functools
import math

import jax
import jax.numpy as jnp
from jax import lax
from jax.experimental import pallas as pl
from jax.experimental.pallas import tpu as pltpu
from jax.sharding import PartitionSpec as P

HEAD_DIM = 128
REACH = 8
AXES = ("section", "attn")
NEG = -1e30
SCALE = HEAD_DIM ** -0.5 * math.log2(math.e)
HEADS_STEP = 4
VMEM_BYTES = 16 * 2**20
HIGH = 2.0 ** 60
barrier = lax.optimization_barrier


def scores(q, k):
    return lax.dot_general(q, k, (((1,), (1,)), ((), ())), preferred_element_type=jnp.float32)


def heads_of(ref, step, count):
    at = pl.multiple_of(step * (count * HEAD_DIM), HEAD_DIM)
    return [ref[:, pl.ds(at + i * HEAD_DIM, HEAD_DIM)] for i in range(count)]


def put_head(ref, step, count, i, value):
    at = pl.multiple_of(step * (count * HEAD_DIM), HEAD_DIM)
    ref[:, pl.ds(at + i * HEAD_DIM, HEAD_DIM)] = value


def with_ones(v, ok):
    return jnp.concatenate([v * ok, ok], axis=1)


def own_kernel(group, info, q_ref, start_ref, k_ref, v_ref, acc_ref, top_ref, total_ref):
    rows = q_ref.shape[0]
    count = HEADS_STEP * group

    def step(j, _):
        start = start_ref[...]
        at = lax.broadcasted_iota(jnp.int32, (rows, rows), 1)
        row = lax.broadcasted_iota(jnp.int32, (rows, rows), 0)
        allowed = (at <= row) & (at + info[0] >= start)
        sees_earlier = jnp.broadcast_to(start, (rows, HEAD_DIM)) <= info[1]
        qs = heads_of(q_ref, j, count)
        ks, vs = heads_of(k_ref, j, HEADS_STEP), heads_of(v_ref, j, HEADS_STEP)
        for i in range(count):
            s = jnp.where(allowed, scores(qs[i], ks[i // group]), NEG)
            top = jnp.max(s, axis=1, keepdims=True)
            w = jnp.exp2((s - top) * SCALE).astype(jnp.bfloat16)
            v = vs[i // group]
            both = jnp.dot(w, with_ones(v, jnp.ones_like(v)), preferred_element_type=jnp.float32)
            put_head(acc_ref, j, count, i, both[:, :HEAD_DIM])
            total_ref[j * count + i] = both[:, HEAD_DIM:]
            top_ref[j * count + i] = jnp.where(sees_earlier, jnp.broadcast_to(top, (rows, HEAD_DIM)), -NEG)
        return 0

    lax.fori_loop(0, k_ref.shape[1] // HEAD_DIM // HEADS_STEP, step, 0)


def far_kernel(group, choose, last, info, q_ref, acc_in, top_in, total_in, *refs):
    rows = q_ref.shape[0]
    if last:
        refs, (hbm, acc_out, sems) = refs[:-3], refs[-3:]
    else:
        refs, (acc_out, top_out, total_out) = refs[:-3], refs[-3:]
    count = HEADS_STEP * group
    steps = refs[0].shape[1] // HEAD_DIM // HEADS_STEP
    needed = info[1] > 0

    def put(j, i, total, out, top=None):
        if last:
            out = (out / total).astype(jnp.bfloat16)
        else:
            if top is not None:
                top_out[j * count + i] = top
            total_out[j * count + i] = total
        put_head(acc_out, j, count, i, out)

    def attend(j, exact):
        qs, befores = heads_of(q_ref, j, count), heads_of(acc_in, j, count)
        tiles = [heads_of(r, j, HEADS_STEP) for r in refs]
        at = lax.broadcasted_iota(jnp.int32, (rows, HEAD_DIM), 0)
        high = None
        for h in range(HEADS_STEP):
            ks, vs = choose(info[0], [t[h] for t in tiles])
            places = [info[3 + n] for n in range(len(ks))]
            k = jnp.concatenate(ks, axis=0)
            ok = [jnp.where(at + place >= info[2], 1.0, 0.0).astype(jnp.bfloat16) for place in places]
            v = jnp.concatenate([with_ones(v, o) for v, o in zip(vs, ok)], axis=0)
            for i in range(h * group, (h + 1) * group):
                s = scores(qs[i], k)
                top, total, before = top_in[j * count + i], total_in[j * count + i], befores[i]
                if exact:
                    key = lax.broadcasted_iota(jnp.int32, (rows, rows), 1)
                    allowed = jnp.concatenate([key + place >= info[2] for place in places], axis=1)
                    s = jnp.where(allowed, s, NEG)
                    new = jnp.maximum(top, jnp.max(s, axis=1, keepdims=True))
                    back = jnp.exp2((top - new) * SCALE)
                    top, total, before = new, total * back, before * back
                w = []
                for n in range(k.shape[0] // HEAD_DIM):
                    part = jnp.exp2((s[:, n * HEAD_DIM:(n + 1) * HEAD_DIM] - top) * SCALE).astype(jnp.bfloat16)
                    w.append(part)
                    if not exact:
                        high = part if high is None else jnp.maximum(high, part)
                both = jnp.dot(jnp.concatenate(w, axis=1), v, preferred_element_type=jnp.float32)
                put(j, i, total + both[:, HEAD_DIM:], both[:, :HEAD_DIM] + before, top if exact else None)
        return high

    def step(j, _):
        @pl.when(needed)
        def _():
            high = attend(j, False)

            @pl.when(jnp.max(high.astype(jnp.float32)) > HIGH)
            def _():
                attend(j, True)

        @pl.when(jnp.logical_not(needed))
        def _():
            for i, before in enumerate(heads_of(acc_in, j, count)):
                put(j, i, total_in[j * count + i], before)

        if last:
            part(j).start()
        return 0

    def part(j):
        width = count * HEAD_DIM
        columns = pl.ds(pl.multiple_of(j * width, width), width)
        return pltpu.make_async_copy(acc_out.at[:, columns], hbm.at[:, columns], sems.at[j])

    lax.fori_loop(0, steps, step, 0)
    if last:
        for j in range(steps):
            part(j).wait()


def pick(plane, at0, at1, at2, at3):
    return jnp.where(plane == 0, at0, jnp.where(plane == 1, at1, jnp.where(plane == 2, at2, at3)))


def choose_first(core, tiles):
    mate_k, mate_v, odd_k, odd_v = tiles
    return (jnp.where(core == 1, mate_k, odd_k),), (jnp.where(core == 1, mate_v, odd_v),)


def choose_middle(plane, tiles):
    def half(x1, y1, x2, y2, z2):
        pk, pv = pick(plane, x2, x2, y2, x2), pick(plane, z2, x1, y1, x1)
        qk, qv = pick(plane, y2, y2, x2, y2), pick(plane, z2, z2, z2, y1)
        return pk, pv, qk, qv
    a, b = half(*tiles[:5]), half(*tiles[5:])
    return (a[0], b[0], a[2], b[2]), (a[1], b[1], a[3], b[3])


def choose_last(plane, tiles):
    def half(z1, y2, x3, y3, z3):
        pk, pv = pick(plane, y2, x3, x3, x3), pick(plane, z3, y3, y3, y3)
        qk, qv = pick(plane, x3, z1, z1, z1), pick(plane, y3, z3, z3, z3)
        return pk, pv, qk, qv
    a, b = half(*tiles[:5]), half(*tiles[5:])
    return (a[0], b[0], a[2], b[2]), (a[1], b[1], a[3], b[3])


def call(kernel, info, q, start, carry, pieces, last, keys):
    rows, width = q.shape
    steps = pieces[0].shape[1] // HEAD_DIM // HEADS_STEP
    group = width // pieces[0].shape[1]
    vmem = pl.BlockSpec(memory_space=pltpu.VMEM)
    arrays = [q, *start, *carry, *pieces]
    if last:
        out_shape = [jax.ShapeDtypeStruct(q.shape, jnp.bfloat16)]
        scratch = [pltpu.VMEM(q.shape, jnp.bfloat16), pltpu.SemaphoreType.DMA((steps,))]
    else:
        out_shape = [jax.ShapeDtypeStruct(q.shape, jnp.float32)]
        out_shape += [jax.ShapeDtypeStruct((width // HEAD_DIM, rows, HEAD_DIM), jnp.float32)] * 2
        scratch = []
    return pl.pallas_call(
        functools.partial(kernel, group),
        in_specs=[pl.BlockSpec(memory_space=pltpu.SMEM)] + [vmem] * len(arrays),
        out_specs=[pl.BlockSpec(memory_space=pl.ANY) if last else vmem] * len(out_shape),
        out_shape=out_shape,
        scratch_shapes=scratch,
        input_output_aliases={3: 1} if carry and not last else {},
        cost_estimate=pl.CostEstimate(
            flops=8 * rows * keys * width, bytes_accessed=4 * rows * width, transcendentals=0
        ),
        compiler_params=pltpu.CompilerParams(vmem_limit_bytes=VMEM_BYTES),
    )(info, *arrays)


def shards(queries, keys, values, doc_ids):
    rows = queries.shape[0]
    chips, cores = lax.axis_size("section"), lax.axis_size("attn")
    chip, core = lax.axis_index("section"), lax.axis_index("attn")
    owner = chip * cores + core
    plane, odd_x, odd_y = chip % 4, chip % 2, (chip // 2) % 2

    def routes(target):
        return [(c * cores + k, target(c) * cores + k) for c in range(chips) for k in range(cores)]

    along = {"x": routes(lambda c: c ^ 1), "y": routes(lambda c: c ^ 2), "z": routes(lambda c: (c + 4) % chips)}
    along["mate"] = [(c * cores + k, c * cores + 1 - k) for c in range(chips) for k in range(cores)]

    def send(array, way):
        return lax.ppermute(array, AXES, along[way])

    def swap(*arrays):
        return tuple(send(a, "mate") for a in arrays)

    first = owner * rows
    span = min(REACH * rows, doc_ids.shape[0])
    low = jnp.maximum(first - (REACH - 1) * rows, 0)
    window = lax.dynamic_slice_in_dim(doc_ids, low, span)
    query_doc = lax.dynamic_slice_in_dim(doc_ids, first, rows)
    start = low + jnp.sum((window[None, :] < query_doc[:, None]).astype(jnp.int32), axis=1, keepdims=True)
    none = jnp.int32(-(2**30))

    def place(device, ok=True):
        return jnp.where((device >= 0) & (device < owner) & ok, device * rows, none)

    def info_of(choice, places):
        newest = functools.reduce(jnp.maximum, places)
        needed = (newest + rows > start[0, 0]).astype(jnp.int32)
        return jnp.stack([choice, needed, start[0, 0]] + places)

    def halves(back):
        base = (chip - back) * cores
        return [place(base + core), place(base + 1 - core)]

    own_info = jnp.stack([first, start[0, 0]])
    first_info = info_of(core, [jnp.where(core == 1, place(owner - 1), place(owner - 7, plane == 0))])
    q_places = [jnp.where(plane == 0, none, p) for p in halves(pick(plane, 0, 2, 3, 2))]
    middle_info = info_of(plane, halves(pick(plane, 3, 1, 2, 1)) + q_places)
    last_info = info_of(plane, halves(pick(plane, 2, 3, 1, 3)) + halves(pick(plane, 1, 4, 4, 4)))

    w = jnp.where
    mate_k, mate_v = swap(keys, values)
    x1, y1 = send(values, "x"), send(values, "y")
    z1 = send(w((plane == 0) & (core == 0), mate_v, keys), "z")
    carry = call(own_kernel, own_info, queries, (start,), (), [keys, values], False, rows)
    x1, y1, z1, mate_k, mate_v, first_info, middle_info, last_info, *carry = barrier(
        (x1, y1, z1, mate_k, mate_v, first_info, middle_info, last_info, *carry)
    )
    x2 = send(w(odd_x == 0, keys, z1), "x")
    y2 = send(w(odd_y == 0, keys, z1), "y")
    z2 = send(w(plane == 1, y1, x1), "z")
    x1s, y1s, z1s = swap(x1, y1, z1)
    carry = call(
        lambda group, *refs: far_kernel(group, choose_first, False, *refs),
        first_info, queries, (), carry, [mate_k, mate_v, z1s, z1], False, rows,
    )
    x2, y2, z2, *carry = barrier((x2, y2, z2, *carry))
    x3 = send(y2, "x")
    y3 = send(w(odd_y == 0, x1, z2), "y")
    z3 = send(w(plane == 0, y1, values), "z")
    x2s, y2s, z2s = swap(x2, y2, z2)
    carry = call(
        lambda group, *refs: far_kernel(group, choose_middle, False, *refs),
        middle_info, queries, (), carry,
        [x1, y1, x2, y2, z2, x1s, y1s, x2s, y2s, z2s], False, 4 * rows,
    )
    x3, y3, z3, *carry = barrier((x3, y3, z3, *carry))
    x3s, y3s, z3s = swap(x3, y3, z3)
    (out,) = call(
        lambda group, *refs: far_kernel(group, choose_last, True, *refs),
        last_info, queries, (), carry,
        [z1, y2, x3, y3, z3, z1s, y2s, x3s, y3s, z3s], True, 4 * rows,
    )
    return out


def solution(mesh):
    split = P(AXES, None)
    return jax.shard_map(
        shards, mesh=mesh, in_specs=(split, split, split, P()), out_specs=split, check_vma=False
    )
```

```python
import functools
import math

import jax
import jax.numpy as jnp
from jax import lax
from jax.experimental import pallas as pl
from jax.experimental.pallas import tpu as pltpu
from jax.sharding import PartitionSpec as P

HEAD_DIM = 128
REACH = 8
AXES = ("section", "attn")
NEG = -1e30
SCALE = HEAD_DIM ** -0.5 * math.log2(math.e)
HEADS_STEP = 4
VMEM_BYTES = 16 * 2**20
HIGH = 2.0 ** 60
barrier = lax.optimization_barrier


def scores(q, k):
    return lax.dot_general(q, k, (((1,), (1,)), ((), ())), preferred_element_type=jnp.float32)


def heads_of(ref, step, count):
    at = pl.multiple_of(step * (count * HEAD_DIM), HEAD_DIM)
    return [ref[:, pl.ds(at + i * HEAD_DIM, HEAD_DIM)] for i in range(count)]


def put_head(ref, step, count, i, value):
    at = pl.multiple_of(step * (count * HEAD_DIM), HEAD_DIM)
    ref[:, pl.ds(at + i * HEAD_DIM, HEAD_DIM)] = value


def with_ones(v, ok):
    return jnp.concatenate([v * ok, ok], axis=1)


def where_am_i(ids, docs_ref, rows):
    chip, core = ids[0], ids[1]
    first = (chip * ids[2] + core) * rows
    head = docs_ref[pl.ds(first // HEAD_DIM, 1), :][:, :1]
    earlier = (docs_ref[...] < head).astype(jnp.int32)
    return chip, core, first, jnp.sum(earlier), head


def own_kernel(group, ids, docs_ref, q_ref, k_ref, v_ref, acc_ref, top_ref, total_ref):
    rows = q_ref.shape[0]
    count = HEADS_STEP * group
    _, _, first, _, head = where_am_i(ids, docs_ref, rows)
    tiles = [docs_ref[pl.ds(first // HEAD_DIM + i, 1), :] for i in range(rows // HEAD_DIM)]
    across = jnp.concatenate(tiles, axis=1)
    down = jnp.concatenate([jnp.broadcast_to(t, (HEAD_DIM, HEAD_DIM)).T for t in tiles], axis=0)
    same = jnp.concatenate([down] * (rows // HEAD_DIM), axis=1) == across
    at = lax.broadcasted_iota(jnp.int32, (rows, rows), 1)
    row = lax.broadcasted_iota(jnp.int32, (rows, rows), 0)
    bias = jnp.where(same & (at <= row), 0.0, NEG)
    sees_earlier = down == head

    def step(j, _):
        qs = heads_of(q_ref, j, count)
        ks, vs = heads_of(k_ref, j, HEADS_STEP), heads_of(v_ref, j, HEADS_STEP)
        for i in range(count):
            s = scores(qs[i], ks[i // group]) + bias
            top = jnp.max(s, axis=1, keepdims=True)
            w = jnp.exp2((s - top) * SCALE).astype(jnp.bfloat16)
            v = vs[i // group]
            both = jnp.dot(w, with_ones(v, jnp.ones_like(v)), preferred_element_type=jnp.float32)
            put_head(acc_ref, j, count, i, both[:, :HEAD_DIM])
            total_ref[j * count + i] = both[:, HEAD_DIM:]
            top_ref[j * count + i] = jnp.where(sees_earlier, jnp.broadcast_to(top, (rows, HEAD_DIM)), -NEG)
        return 0

    lax.fori_loop(0, k_ref.shape[1] // HEAD_DIM // HEADS_STEP, step, 0)


def far_kernel(choose, devices, last, group, ids, docs_ref, q_ref, acc_in, top_in, total_in, *refs):
    rows = q_ref.shape[0]
    chip, core, first, start, _ = where_am_i(ids, docs_ref, rows)
    plane, owner = chip % 4, first // rows
    places = [jnp.where((d >= 0) & (d < owner), d * rows, -(2**30)) for d in devices(plane, core, chip * ids[2])]
    if last:
        refs, (hbm, acc_out, sems) = refs[:-3], refs[-3:]
    else:
        refs, (acc_out, top_out, total_out) = refs[:-3], refs[-3:]
    count = HEADS_STEP * group
    steps = refs[0].shape[1] // HEAD_DIM // HEADS_STEP
    needed = functools.reduce(jnp.maximum, places) + rows > start

    def put(j, i, total, out, top=None):
        if last:
            out = (out / total).astype(jnp.bfloat16)
        else:
            if top is not None:
                top_out[j * count + i] = top
            total_out[j * count + i] = total
        put_head(acc_out, j, count, i, out)

    def attend(j, exact):
        qs, befores = heads_of(q_ref, j, count), heads_of(acc_in, j, count)
        tiles = [heads_of(r, j, HEADS_STEP) for r in refs]
        at = lax.broadcasted_iota(jnp.int32, (rows, HEAD_DIM), 0)
        high = None
        for h in range(HEADS_STEP):
            ks, vs = choose(plane, core, [t[h] for t in tiles])
            k = jnp.concatenate(ks, axis=0)
            ok = [jnp.where(at + place >= start, 1.0, 0.0).astype(jnp.bfloat16) for place in places]
            v = jnp.concatenate([with_ones(v, o) for v, o in zip(vs, ok)], axis=0)
            for i in range(h * group, (h + 1) * group):
                s = scores(qs[i], k)
                top, total, before = top_in[j * count + i], total_in[j * count + i], befores[i]
                if exact:
                    key = lax.broadcasted_iota(jnp.int32, (rows, rows), 1)
                    allowed = jnp.concatenate([key + place >= start for place in places], axis=1)
                    s = jnp.where(allowed, s, NEG)
                    new = jnp.maximum(top, jnp.max(s, axis=1, keepdims=True))
                    back = jnp.exp2((top - new) * SCALE)
                    top, total, before = new, total * back, before * back
                w = []
                for n in range(k.shape[0] // HEAD_DIM):
                    part = jnp.exp2((s[:, n * HEAD_DIM:(n + 1) * HEAD_DIM] - top) * SCALE).astype(jnp.bfloat16)
                    w.append(part)
                    if not exact:
                        high = part if high is None else jnp.maximum(high, part)
                both = jnp.dot(jnp.concatenate(w, axis=1), v, preferred_element_type=jnp.float32)
                put(j, i, total + both[:, HEAD_DIM:], both[:, :HEAD_DIM] + before, top if exact else None)
        return high

    def step(j, _):
        @pl.when(needed)
        def _():
            high = attend(j, False)

            @pl.when(jnp.max(high.astype(jnp.float32)) > HIGH)
            def _():
                attend(j, True)

        @pl.when(jnp.logical_not(needed))
        def _():
            for i, before in enumerate(heads_of(acc_in, j, count)):
                put(j, i, total_in[j * count + i], before)

        if last:
            part(j).start()
        return 0

    def part(j):
        width = count * HEAD_DIM
        columns = pl.ds(pl.multiple_of(j * width, width), width)
        return pltpu.make_async_copy(acc_out.at[:, columns], hbm.at[:, columns], sems.at[j])

    lax.fori_loop(0, steps, step, 0)
    if last:
        for j in range(steps):
            part(j).wait()


def pick(plane, at0, at1, at2, at3):
    return jnp.where(plane == 0, at0, jnp.where(plane == 1, at1, jnp.where(plane == 2, at2, at3)))


def choose_first(plane, core, tiles):
    mate_k, mate_v, odd_k, odd_v = tiles
    return (jnp.where(core == 1, mate_k, odd_k),), (jnp.where(core == 1, mate_v, odd_v),)


def devices_first(plane, core, base):
    return (jnp.where(core == 1, base, jnp.where(plane == 0, base - 7, -1)),)


def choose_middle(plane, core, tiles):
    def half(x1, y1, x2, y2, z2):
        pk, pv = pick(plane, x2, x2, y2, x2), pick(plane, z2, x1, y1, x1)
        qk, qv = pick(plane, y2, y2, x2, y2), pick(plane, z2, z2, z2, y1)
        return (pk, qk), (pv, qv)
    a, b = half(*tiles[:5]), half(*tiles[5:])
    return a[0] + b[0], a[1] + b[1]


def devices_middle(plane, core, base):
    p = base - 2 * pick(plane, 3, 1, 2, 1)
    q = pick(plane, -8, base - 4, base - 6, base - 4)
    return p + core, q + core, p + 1 - core, q + 1 - core


def choose_last(plane, core, tiles):
    z1, y2, x3, y3, z3 = tiles
    pk, pv = pick(plane, y2, x3, x3, x3), pick(plane, z3, y3, y3, y3)
    qk, qv = pick(plane, x3, z1, z1, z1), pick(plane, y3, z3, z3, z3)
    return (pk, qk), (pv, qv)


def devices_last(mates, plane, core, base):
    part = 1 - core if mates else core
    return base - 2 * pick(plane, 2, 3, 1, 3) + part, base - 2 * pick(plane, 1, 4, 4, 4) + part


def call(kernel, ids, docs, q, carry, pieces, keys, last=False):
    rows, width = q.shape
    steps = pieces[0].shape[1] // HEAD_DIM // HEADS_STEP
    group = width // pieces[0].shape[1]
    vmem = pl.BlockSpec(memory_space=pltpu.VMEM)
    arrays = [docs, q, *carry, *pieces]
    if last:
        out_shape = [jax.ShapeDtypeStruct(q.shape, jnp.bfloat16)]
        scratch = [pltpu.VMEM(q.shape, jnp.bfloat16), pltpu.SemaphoreType.DMA((steps,))]
    else:
        out_shape = [jax.ShapeDtypeStruct(q.shape, jnp.float32)]
        out_shape += [jax.ShapeDtypeStruct((width // HEAD_DIM, rows, HEAD_DIM), jnp.float32)] * 2
        scratch = []
    return pl.pallas_call(
        functools.partial(kernel, group),
        in_specs=[pl.BlockSpec(memory_space=pltpu.SMEM)] + [vmem] * len(arrays),
        out_specs=[pl.BlockSpec(memory_space=pl.ANY) if last else vmem] * len(out_shape),
        out_shape=out_shape,
        scratch_shapes=scratch,
        input_output_aliases={4: 1} if carry and not last else {},
        cost_estimate=pl.CostEstimate(
            flops=8 * rows * keys * width, bytes_accessed=4 * rows * width, transcendentals=0
        ),
        compiler_params=pltpu.CompilerParams(vmem_limit_bytes=VMEM_BYTES),
    )(ids, *arrays)


def shards(queries, keys, values, doc_ids):
    rows = queries.shape[0]
    chips, cores = lax.axis_size("section"), lax.axis_size("attn")
    chip, core = lax.axis_index("section"), lax.axis_index("attn")
    plane, odd_x, odd_y = chip % 4, chip % 2, (chip // 2) % 2

    def routes(target):
        return [
            (c * cores + k, at * cores + to)
            for c in range(chips) for k in range(cores) for at, to in [target(c, k)]
        ]

    def up(c):
        return (c + 4) % chips

    along = {
        "x": routes(lambda c, k: (c ^ 1, k)),
        "y": routes(lambda c, k: (c ^ 2, k)),
        "z": routes(lambda c, k: (up(c), k)),
        "mate": routes(lambda c, k: (c, 1 - k)),
        "z_odd": routes(lambda c, k: (c, k) if c % 4 == 0 and k == 0 else (up(c), k)),
        "odd": routes(lambda c, k: (c, k) if c % 4 else ((up(c), 0) if k else (c, 1))),
    }

    def send(array, way):
        return lax.ppermute(array, AXES, along[way])

    def swap(*arrays):
        return tuple(send(a, "mate") for a in arrays)

    ids = jnp.stack([chip, core, jnp.int32(cores)])
    docs = doc_ids.reshape(-1, HEAD_DIM)
    w = jnp.where

    def far(choose, devices, carry, pieces, keys, last=False):
        kernel = functools.partial(far_kernel, choose, devices, last)
        return call(kernel, ids, docs, queries, carry, pieces, keys, last)

    z1 = send(keys, "z_odd")
    x1, y1 = send(values, "x"), send(values, "y")
    odd_v = send(values, "odd")
    mate_k, mate_v = swap(keys, values)
    carry = call(own_kernel, ids, docs, queries, (), [keys, values], rows)
    z1, odd_v, *carry = barrier((z1, odd_v, *carry))
    x2 = send(w(odd_x == 0, keys, z1), "x")
    y2 = send(w(odd_y == 0, keys, z1), "y")
    z2 = send(w(plane == 1, y1, x1), "z")
    x1s, y1s, z1s = swap(x1, y1, z1)
    carry = far(choose_first, devices_first, carry, [mate_k, mate_v, z1s, odd_v], rows)
    y2, z2, y1, *carry = barrier((y2, z2, y1, *carry))
    x3 = send(y2, "x")
    y3 = send(w(odd_y == 0, x1, z2), "y")
    z3 = send(w(plane == 0, y1, values), "z")
    x2s, y2s, z2s = swap(x2, y2, z2)
    carry = far(
        choose_middle, devices_middle, carry, [x1, y1, x2, y2, z2, x1s, y1s, x2s, y2s, z2s], 4 * rows
    )
    x3, y3, z3, *carry = barrier((x3, y3, z3, *carry))
    x3s, y3s, z3s = swap(x3, y3, z3)
    carry = far(choose_last, functools.partial(devices_last, False), carry, [z1, y2, x3, y3, z3], 2 * rows)
    (out,) = far(
        choose_last, functools.partial(devices_last, True), carry, [z1s, y2s, x3s, y3s, z3s], 2 * rows, True
    )
    return out


def solution(mesh):
    split = P(AXES, None)
    return jax.shard_map(
        shards, mesh=mesh, in_specs=(split, split, split, P()), out_specs=split, check_vma=False
    )
```

```python
import functools
import math

import jax
import jax.numpy as jnp
from jax import lax
from jax.experimental import pallas as pl
from jax.experimental.pallas import tpu as pltpu
from jax.sharding import PartitionSpec as P

HEAD_DIM = 128
REACH = 8
AXES = ("section", "attn")
NEG = -1e30
SCALE = HEAD_DIM ** -0.5 * math.log2(math.e)
HEADS_STEP = 4
VMEM_BYTES = 16 * 2**20
HIGH = 2.0 ** 60
barrier = lax.optimization_barrier


def scores(q, k):
    return lax.dot_general(q, k, (((1,), (1,)), ((), ())), preferred_element_type=jnp.float32)


def heads_of(ref, step, count):
    at = pl.multiple_of(step * (count * HEAD_DIM), HEAD_DIM)
    return [ref[:, pl.ds(at + i * HEAD_DIM, HEAD_DIM)] for i in range(count)]


def put_head(ref, step, count, i, value):
    at = pl.multiple_of(step * (count * HEAD_DIM), HEAD_DIM)
    ref[:, pl.ds(at + i * HEAD_DIM, HEAD_DIM)] = value


def with_ones(v, ok):
    return jnp.concatenate([v * ok, ok], axis=1)


def where_am_i(ids, docs_ref, rows):
    chip, core = ids[0], ids[1]
    first = (chip * ids[2] + core) * rows
    head = docs_ref[pl.ds(first // HEAD_DIM, 1), :][:, :1]
    earlier = (docs_ref[...] < head).astype(jnp.int32)
    return chip, core, first, jnp.sum(earlier), head


def own_kernel(group, ids, docs_ref, q_ref, k_ref, v_ref, acc_ref, top_ref, total_ref):
    rows = q_ref.shape[0]
    count = HEADS_STEP * group
    _, _, first, _, head = where_am_i(ids, docs_ref, rows)
    tiles = [docs_ref[pl.ds(first // HEAD_DIM + i, 1), :] for i in range(rows // HEAD_DIM)]
    across = jnp.concatenate(tiles, axis=1)
    down = jnp.concatenate([jnp.broadcast_to(t, (HEAD_DIM, HEAD_DIM)).T for t in tiles], axis=0)
    same = jnp.concatenate([down] * (rows // HEAD_DIM), axis=1) == across
    at = lax.broadcasted_iota(jnp.int32, (rows, rows), 1)
    row = lax.broadcasted_iota(jnp.int32, (rows, rows), 0)
    bias = jnp.where(same & (at <= row), 0.0, NEG)
    sees_earlier = down == head

    def step(j, _):
        qs = heads_of(q_ref, j, count)
        ks, vs = heads_of(k_ref, j, HEADS_STEP), heads_of(v_ref, j, HEADS_STEP)
        for i in range(count):
            s = scores(qs[i], ks[i // group]) + bias
            top = jnp.max(s, axis=1, keepdims=True)
            w = jnp.exp2((s - top) * SCALE).astype(jnp.bfloat16)
            v = vs[i // group]
            both = jnp.dot(w, with_ones(v, jnp.ones_like(v)), preferred_element_type=jnp.float32)
            put_head(acc_ref, j, count, i, both[:, :HEAD_DIM])
            total_ref[j * count + i] = both[:, HEAD_DIM:]
            top_ref[j * count + i] = jnp.where(sees_earlier, jnp.broadcast_to(top, (rows, HEAD_DIM)), -NEG)
        return 0

    lax.fori_loop(0, k_ref.shape[1] // HEAD_DIM // HEADS_STEP, step, 0)


def far_kernel(choose, devices, last, group, ids, docs_ref, q_ref, acc_in, top_in, total_in, *refs):
    rows = q_ref.shape[0]
    chip, core, first, start, _ = where_am_i(ids, docs_ref, rows)
    plane, owner = chip % 4, first // rows
    places = [jnp.where((d >= 0) & (d < owner), d * rows, -(2**30)) for d in devices(plane, core, chip * ids[2])]
    if last:
        refs, (hbm, acc_out, sems) = refs[:-3], refs[-3:]
    else:
        refs, (acc_out, top_out, total_out) = refs[:-3], refs[-3:]
    count = HEADS_STEP * group
    steps = refs[0].shape[1] // HEAD_DIM // HEADS_STEP
    needed = functools.reduce(jnp.maximum, places) + rows > start

    def put(j, i, total, out, top=None):
        if last:
            out = (out / total).astype(jnp.bfloat16)
        else:
            if top is not None:
                top_out[j * count + i] = top
            total_out[j * count + i] = total
        put_head(acc_out, j, count, i, out)

    def attend(j, exact):
        qs, befores = heads_of(q_ref, j, count), heads_of(acc_in, j, count)
        tiles = [heads_of(r, j, HEADS_STEP) for r in refs]
        at = lax.broadcasted_iota(jnp.int32, (rows, HEAD_DIM), 0)
        high = None
        for h in range(HEADS_STEP):
            ks, vs = choose(plane, core, [t[h] for t in tiles])
            k = jnp.concatenate(ks, axis=0)
            ok = [jnp.where(at + place >= start, 1.0, 0.0).astype(jnp.bfloat16) for place in places]
            v = jnp.concatenate([with_ones(v, o) for v, o in zip(vs, ok)], axis=0)
            for i in range(h * group, (h + 1) * group):
                s = scores(qs[i], k)
                top, total, before = top_in[j * count + i], total_in[j * count + i], befores[i]
                if exact:
                    key = lax.broadcasted_iota(jnp.int32, (rows, rows), 1)
                    allowed = jnp.concatenate([key + place >= start for place in places], axis=1)
                    s = jnp.where(allowed, s, NEG)
                    new = jnp.maximum(top, jnp.max(s, axis=1, keepdims=True))
                    back = jnp.exp2((top - new) * SCALE)
                    top, total, before = new, total * back, before * back
                w = []
                for n in range(k.shape[0] // HEAD_DIM):
                    part = jnp.exp2((s[:, n * HEAD_DIM:(n + 1) * HEAD_DIM] - top) * SCALE).astype(jnp.bfloat16)
                    w.append(part)
                    if not exact:
                        high = part if high is None else jnp.maximum(high, part)
                both = jnp.dot(jnp.concatenate(w, axis=1), v, preferred_element_type=jnp.float32)
                put(j, i, total + both[:, HEAD_DIM:], both[:, :HEAD_DIM] + before, top if exact else None)
        return high

    def step(j, _):
        @pl.when(needed)
        def _():
            high = attend(j, False)

            @pl.when(jnp.max(high.astype(jnp.float32)) > HIGH)
            def _():
                attend(j, True)

        @pl.when(jnp.logical_not(needed))
        def _():
            for i, before in enumerate(heads_of(acc_in, j, count)):
                put(j, i, total_in[j * count + i], before)

        if last:
            part(j).start()
        return 0

    def part(j):
        width = count * HEAD_DIM
        columns = pl.ds(pl.multiple_of(j * width, width), width)
        return pltpu.make_async_copy(acc_out.at[:, columns], hbm.at[:, columns], sems.at[j])

    lax.fori_loop(0, steps, step, 0)
    if last:
        for j in range(steps):
            part(j).wait()


def pick(plane, at0, at1, at2, at3):
    return jnp.where(plane == 0, at0, jnp.where(plane == 1, at1, jnp.where(plane == 2, at2, at3)))


def choose_first(plane, core, tiles):
    mate_k, mate_v, odd_k, odd_v = tiles
    return (jnp.where(core == 1, mate_k, odd_k),), (jnp.where(core == 1, mate_v, odd_v),)


def devices_first(plane, core, base):
    return (jnp.where(core == 1, base, jnp.where(plane == 0, base - 7, -1)),)


def choose_middle(plane, core, tiles):
    def half(x1, y1, x2, y2, z2):
        pk, pv = pick(plane, x2, x2, y2, x2), pick(plane, z2, x1, y1, x1)
        qk, qv = pick(plane, y2, y2, x2, y2), pick(plane, z2, z2, z2, y1)
        return (pk, qk), (pv, qv)
    a, b = half(*tiles[:5]), half(*tiles[5:])
    return a[0] + b[0], a[1] + b[1]


def devices_middle(plane, core, base):
    p = base - 2 * pick(plane, 3, 1, 2, 1)
    q = pick(plane, -8, base - 4, base - 6, base - 4)
    return p + core, q + core, p + 1 - core, q + 1 - core


def choose_last(plane, core, tiles):
    z1, y2, x3, y3, z3 = tiles
    pk, pv = pick(plane, y2, x3, x3, x3), pick(plane, z3, y3, y3, y3)
    qk, qv = pick(plane, x3, z1, z1, z1), pick(plane, y3, z3, z3, z3)
    return (pk, qk), (pv, qv)


def devices_last(mates, plane, core, base):
    part = 1 - core if mates else core
    return base - 2 * pick(plane, 2, 3, 1, 3) + part, base - 2 * pick(plane, 1, 4, 4, 4) + part


def call(kernel, ids, docs, q, carry, pieces, keys, last=False):
    rows, width = q.shape
    steps = pieces[0].shape[1] // HEAD_DIM // HEADS_STEP
    group = width // pieces[0].shape[1]
    vmem = pl.BlockSpec(memory_space=pltpu.VMEM)
    arrays = [docs, q, *carry, *pieces]
    if last:
        out_shape = [jax.ShapeDtypeStruct(q.shape, jnp.bfloat16)]
        scratch = [pltpu.VMEM(q.shape, jnp.bfloat16), pltpu.SemaphoreType.DMA((steps,))]
    else:
        out_shape = [jax.ShapeDtypeStruct(q.shape, jnp.float32)]
        out_shape += [jax.ShapeDtypeStruct((width // HEAD_DIM, rows, HEAD_DIM), jnp.float32)] * 2
        scratch = []
    return pl.pallas_call(
        functools.partial(kernel, group),
        in_specs=[pl.BlockSpec(memory_space=pltpu.SMEM)] + [vmem] * len(arrays),
        out_specs=[pl.BlockSpec(memory_space=pl.ANY) if last else vmem] * len(out_shape),
        out_shape=out_shape,
        scratch_shapes=scratch,
        input_output_aliases={4: 1} if carry and not last else {},
        cost_estimate=pl.CostEstimate(
            flops=8 * rows * keys * width, bytes_accessed=4 * rows * width, transcendentals=0
        ),
        compiler_params=pltpu.CompilerParams(vmem_limit_bytes=VMEM_BYTES),
    )(ids, *arrays)


def shards(queries, keys, values, doc_ids):
    rows = queries.shape[0]
    chips, cores = lax.axis_size("section"), lax.axis_size("attn")
    chip, core = lax.axis_index("section"), lax.axis_index("attn")
    plane, odd_x, odd_y = chip % 4, chip % 2, (chip // 2) % 2

    def routes(target):
        return [
            (c * cores + k, at * cores + to)
            for c in range(chips) for k in range(cores) for at, to in [target(c, k)]
        ]

    def up(c):
        return (c + 4) % chips

    along = {
        "x": routes(lambda c, k: (c ^ 1, k)),
        "y": routes(lambda c, k: (c ^ 2, k)),
        "z": routes(lambda c, k: (up(c), k)),
        "mate": routes(lambda c, k: (c, 1 - k)),
    }

    def send(array, way):
        return lax.ppermute(array, AXES, along[way])

    def swap(*arrays):
        return tuple(send(a, "mate") for a in arrays)

    ids = jnp.stack([chip, core, jnp.int32(cores)])
    docs = doc_ids.reshape(-1, HEAD_DIM)
    w = jnp.where

    def far(choose, devices, carry, pieces, keys, last=False):
        kernel = functools.partial(far_kernel, choose, devices, last)
        return call(kernel, ids, docs, queries, carry, pieces, keys, last)

    mate_v = send(values, "mate")
    x1, y1 = send(values, "x"), send(values, "y")
    z1 = send(w((plane == 0) & (core == 0), mate_v, keys), "z")
    mate_k = send(keys, "mate")
    x1, y1 = barrier((x1, y1))
    up2 = w(plane == 1, y1, x1)
    z2 = send(up2, "z")
    z1, up2, mate_k, mate_v = barrier((z1, up2, mate_k, mate_v))
    x2 = send(w(odd_x == 0, keys, z1), "x")
    y2 = send(w(odd_y == 0, keys, z1), "y")
    x1s, y1s, z1s = swap(x1, y1, z1)
    carry = call(own_kernel, ids, docs, queries, (), [keys, values], rows)
    carry = far(choose_first, devices_first, carry, [mate_k, mate_v, z1s, z1], rows)
    y2, z2, y1, *carry = barrier((y2, z2, y1, *carry))
    up3, side3 = w(plane == 0, y1, values), w(odd_y == 0, x1, z2)
    z3, x3, y3 = send(up3, "z"), send(y2, "x"), send(side3, "y")
    x2s, y2s, z2s = swap(x2, y2, z2)
    carry = far(
        choose_middle, devices_middle, carry, [x1, y1, x2, y2, z2, x1s, y1s, x2s, y2s, z2s], 4 * rows
    )
    x3, y3, z3, *carry = barrier((x3, y3, z3, *carry))
    x3s, y3s, z3s = swap(x3, y3, z3)
    carry = far(choose_last, functools.partial(devices_last, False), carry, [z1, y2, x3, y3, z3], 2 * rows)
    (out,) = far(
        choose_last, functools.partial(devices_last, True), carry, [z1s, y2s, x3s, y3s, z3s], 2 * rows, True
    )
    return out


def solution(mesh):
    split = P(AXES, None)
    return jax.shard_map(
        shards, mesh=mesh, in_specs=(split, split, split, P()), out_specs=split, check_vma=False
    )
```

```python
import functools
import math

import jax
import jax.numpy as jnp
from jax import lax
from jax.experimental import pallas as pl
from jax.experimental.pallas import tpu as pltpu
from jax.sharding import PartitionSpec as P

HEAD_DIM = 128
REACH = 8
AXES = ("section", "attn")
NEG = -1e30
SCALE = HEAD_DIM ** -0.5 * math.log2(math.e)
HEADS_STEP = 4
VMEM_BYTES = 16 * 2**20
LOAD_BYTES = 60 * 2**20
HIGH = 2.0 ** 60
barrier = lax.optimization_barrier


def scores(q, k):
    return lax.dot_general(q, k, (((1,), (1,)), ((), ())), preferred_element_type=jnp.float32)


def heads_of(ref, step, count):
    at = pl.multiple_of(step * (count * HEAD_DIM), HEAD_DIM)
    return [ref[:, pl.ds(at + i * HEAD_DIM, HEAD_DIM)] for i in range(count)]


def put_head(ref, step, count, i, value):
    at = pl.multiple_of(step * (count * HEAD_DIM), HEAD_DIM)
    ref[:, pl.ds(at + i * HEAD_DIM, HEAD_DIM)] = value


def with_ones(v, ok):
    return jnp.concatenate([v * ok, ok], axis=1)


def where_am_i(ids, docs_ref, rows):
    chip, core = ids[0], ids[1]
    first = (chip * ids[2] + core) * rows
    head = docs_ref[pl.ds(first // HEAD_DIM, 1), :][:, :1]
    earlier = (docs_ref[...] < head).astype(jnp.int32)
    return chip, core, first, jnp.sum(earlier), head


def load_kernel(*refs):
    count = len(refs) // 2
    copies = [pltpu.make_async_copy(refs[i], refs[count + i], refs[-1].at[i]) for i in range(count)]
    for copy in copies:
        copy.start()
    for copy in copies:
        copy.wait()


def own_kernel(group, ids, docs_ref, q_ref, k_ref, v_ref, acc_ref, top_ref, total_ref):
    rows = q_ref.shape[0]
    count = HEADS_STEP * group
    _, _, first, _, head = where_am_i(ids, docs_ref, rows)
    tiles = [docs_ref[pl.ds(first // HEAD_DIM + i, 1), :] for i in range(rows // HEAD_DIM)]
    across = jnp.concatenate(tiles, axis=1)
    down = jnp.concatenate([jnp.broadcast_to(t, (HEAD_DIM, HEAD_DIM)).T for t in tiles], axis=0)
    same = jnp.concatenate([down] * (rows // HEAD_DIM), axis=1) == across
    at = lax.broadcasted_iota(jnp.int32, (rows, rows), 1)
    row = lax.broadcasted_iota(jnp.int32, (rows, rows), 0)
    bias = jnp.where(same & (at <= row), 0.0, NEG)
    sees_earlier = down == head

    def step(j, _):
        qs = heads_of(q_ref, j, count)
        ks, vs = heads_of(k_ref, j, HEADS_STEP), heads_of(v_ref, j, HEADS_STEP)
        for i in range(count):
            s = scores(qs[i], ks[i // group]) + bias
            top = jnp.max(s, axis=1, keepdims=True)
            w = jnp.exp2((s - top) * SCALE).astype(jnp.bfloat16)
            v = vs[i // group]
            both = jnp.dot(w, with_ones(v, jnp.ones_like(v)), preferred_element_type=jnp.float32)
            put_head(acc_ref, j, count, i, both[:, :HEAD_DIM])
            total_ref[j * count + i] = both[:, HEAD_DIM:]
            top_ref[j * count + i] = jnp.where(sees_earlier, jnp.broadcast_to(top, (rows, HEAD_DIM)), -NEG)
        return 0

    lax.fori_loop(0, k_ref.shape[1] // HEAD_DIM // HEADS_STEP, step, 0)


def far_kernel(choose, devices, last, group, ids, docs_ref, q_ref, acc_in, top_in, total_in, *refs):
    rows = q_ref.shape[0]
    chip, core, first, start, _ = where_am_i(ids, docs_ref, rows)
    plane, owner = chip % 4, first // rows
    places = [jnp.where((d >= 0) & (d < owner), d * rows, -(2**30)) for d in devices(plane, core, chip * ids[2])]
    if last:
        refs, (hbm, acc_out, sems) = refs[:-3], refs[-3:]
    else:
        refs, (acc_out, top_out, total_out) = refs[:-3], refs[-3:]
    count = HEADS_STEP * group
    steps = refs[0].shape[1] // HEAD_DIM // HEADS_STEP
    needed = functools.reduce(jnp.maximum, places) + rows > start

    def put(j, i, total, out, top=None):
        if last:
            out = (out / total).astype(jnp.bfloat16)
        else:
            if top is not None:
                top_out[j * count + i] = top
            total_out[j * count + i] = total
        put_head(acc_out, j, count, i, out)

    def attend(j, exact):
        qs, befores = heads_of(q_ref, j, count), heads_of(acc_in, j, count)
        tiles = [heads_of(r, j, HEADS_STEP) for r in refs]
        at = lax.broadcasted_iota(jnp.int32, (rows, HEAD_DIM), 0)
        high = None
        for h in range(HEADS_STEP):
            ks, vs = choose(plane, core, [t[h] for t in tiles])
            k = jnp.concatenate(ks, axis=0)
            ok = [jnp.where(at + place >= start, 1.0, 0.0).astype(jnp.bfloat16) for place in places]
            v = jnp.concatenate([with_ones(v, o) for v, o in zip(vs, ok)], axis=0)
            for i in range(h * group, (h + 1) * group):
                s = scores(qs[i], k)
                top, total, before = top_in[j * count + i], total_in[j * count + i], befores[i]
                if exact:
                    key = lax.broadcasted_iota(jnp.int32, (rows, rows), 1)
                    allowed = jnp.concatenate([key + place >= start for place in places], axis=1)
                    s = jnp.where(allowed, s, NEG)
                    new = jnp.maximum(top, jnp.max(s, axis=1, keepdims=True))
                    back = jnp.exp2((top - new) * SCALE)
                    top, total, before = new, total * back, before * back
                w = []
                for n in range(k.shape[0] // HEAD_DIM):
                    part = jnp.exp2((s[:, n * HEAD_DIM:(n + 1) * HEAD_DIM] - top) * SCALE).astype(jnp.bfloat16)
                    w.append(part)
                    if not exact:
                        high = part if high is None else jnp.maximum(high, part)
                both = jnp.dot(jnp.concatenate(w, axis=1), v, preferred_element_type=jnp.float32)
                put(j, i, total + both[:, HEAD_DIM:], both[:, :HEAD_DIM] + before, top if exact else None)
        return high

    def step(j, _):
        @pl.when(needed)
        def _():
            high = attend(j, False)

            @pl.when(jnp.max(high.astype(jnp.float32)) > HIGH)
            def _():
                attend(j, True)

        @pl.when(jnp.logical_not(needed))
        def _():
            for i, before in enumerate(heads_of(acc_in, j, count)):
                put(j, i, total_in[j * count + i], before)

        if last:
            part(j).start()
        return 0

    def part(j):
        width = count * HEAD_DIM
        columns = pl.ds(pl.multiple_of(j * width, width), width)
        return pltpu.make_async_copy(acc_out.at[:, columns], hbm.at[:, columns], sems.at[j])

    lax.fori_loop(0, steps, step, 0)
    if last:
        for j in range(steps):
            part(j).wait()


def pick(plane, at0, at1, at2, at3):
    return jnp.where(plane == 0, at0, jnp.where(plane == 1, at1, jnp.where(plane == 2, at2, at3)))


def choose_first(plane, core, tiles):
    mate_k, mate_v, odd_k, odd_v = tiles
    return (jnp.where(core == 1, mate_k, odd_k),), (jnp.where(core == 1, mate_v, odd_v),)


def devices_first(plane, core, base):
    return (jnp.where(core == 1, base, jnp.where(plane == 0, base - 7, -1)),)


def choose_middle(plane, core, tiles):
    x1, y1, x2, y2, z2 = tiles
    pk, pv = pick(plane, x2, x2, y2, x2), pick(plane, z2, x1, y1, x1)
    qk, qv = pick(plane, y2, y2, x2, y2), pick(plane, z2, z2, z2, y1)
    return (pk, qk), (pv, qv)


def devices_middle(mates, plane, core, base):
    part = 1 - core if mates else core
    return base - 2 * pick(plane, 3, 1, 2, 1) + part, pick(plane, -8, base - 4, base - 6, base - 4) + part


def choose_last(plane, core, tiles):
    z1, y2, x3, y3, z3 = tiles
    pk, pv = pick(plane, y2, x3, x3, x3), pick(plane, z3, y3, y3, y3)
    qk, qv = pick(plane, x3, z1, z1, z1), pick(plane, y3, z3, z3, z3)
    return (pk, qk), (pv, qv)


def devices_last(mates, plane, core, base):
    part = 1 - core if mates else core
    return base - 2 * pick(plane, 2, 3, 1, 3) + part, base - 2 * pick(plane, 1, 4, 4, 4) + part


def call(kernel, ids, docs, q, carry, pieces, keys, last=False):
    rows, width = q.shape
    steps = pieces[0].shape[1] // HEAD_DIM // HEADS_STEP
    group = width // pieces[0].shape[1]
    vmem = pl.BlockSpec(memory_space=pltpu.VMEM)
    arrays = [docs, q, *carry, *pieces]
    if last:
        out_shape = [jax.ShapeDtypeStruct(q.shape, jnp.bfloat16)]
        scratch = [pltpu.VMEM(q.shape, jnp.bfloat16), pltpu.SemaphoreType.DMA((steps,))]
    else:
        out_shape = [jax.ShapeDtypeStruct(q.shape, jnp.float32)]
        out_shape += [jax.ShapeDtypeStruct((width // HEAD_DIM, rows, HEAD_DIM), jnp.float32)] * 2
        scratch = []
    return pl.pallas_call(
        functools.partial(kernel, group),
        in_specs=[pl.BlockSpec(memory_space=pltpu.SMEM)] + [vmem] * len(arrays),
        out_specs=[pl.BlockSpec(memory_space=pl.ANY) if last else vmem] * len(out_shape),
        out_shape=out_shape,
        scratch_shapes=scratch,
        input_output_aliases={4: 1} if carry and not last else {},
        cost_estimate=pl.CostEstimate(
            flops=8 * rows * keys * width, bytes_accessed=4 * rows * width, transcendentals=0
        ),
        compiler_params=pltpu.CompilerParams(vmem_limit_bytes=VMEM_BYTES),
    )(ids, *arrays)


def load(*arrays):
    return pl.pallas_call(
        load_kernel,
        in_specs=[pl.BlockSpec(memory_space=pl.ANY)] * len(arrays),
        out_specs=[pl.BlockSpec(memory_space=pltpu.VMEM)] * len(arrays),
        out_shape=[jax.ShapeDtypeStruct(a.shape, a.dtype) for a in arrays],
        scratch_shapes=[pltpu.SemaphoreType.DMA((len(arrays),))],
        cost_estimate=pl.CostEstimate(flops=0, bytes_accessed=4 * arrays[0].size, transcendentals=0),
        compiler_params=pltpu.CompilerParams(vmem_limit_bytes=LOAD_BYTES),
    )(*arrays)


def shards(queries, keys, values, doc_ids):
    rows = queries.shape[0]
    chips, cores = lax.axis_size("section"), lax.axis_size("attn")
    chip, core = lax.axis_index("section"), lax.axis_index("attn")
    plane, odd_x, odd_y = chip % 4, chip % 2, (chip // 2) % 2

    def routes(target):
        return [
            (c * cores + k, at * cores + to)
            for c in range(chips) for k in range(cores) for at, to in [target(c, k)]
        ]

    def up(c):
        return (c + 4) % chips

    along = {
        "x": routes(lambda c, k: (c ^ 1, k)),
        "y": routes(lambda c, k: (c ^ 2, k)),
        "z": routes(lambda c, k: (up(c), k)),
        "mate": routes(lambda c, k: (c, 1 - k)),
    }

    def send(array, way):
        return lax.ppermute(array, AXES, along[way])

    def swap(*arrays):
        return tuple(send(a, "mate") for a in arrays)

    ids = jnp.stack([chip, core, jnp.int32(cores)])
    docs = doc_ids.reshape(-1, HEAD_DIM)
    w = jnp.where

    def far(choose, devices, carry, pieces, keys, last=False):
        kernel = functools.partial(far_kernel, choose, devices, last)
        return call(kernel, ids, docs, queries, carry, pieces, keys, last)

    mate_v = send(values, "mate")
    x1, y1 = send(values, "x"), send(values, "y")
    mate_k = send(keys, "mate")
    queries, keys, values = load(queries, keys, values)
    z1 = send(w((plane == 0) & (core == 0), mate_v, keys), "z")
    z1, mate_k, mate_v = barrier((z1, mate_k, mate_v))
    across2, side2 = w(odd_x == 0, keys, z1), w(odd_y == 0, keys, z1)
    x2, y2 = send(across2, "x"), send(side2, "y")
    x1, y1, _, _ = barrier((x1, y1, across2, side2))
    z2 = send(w(plane == 1, y1, x1), "z")
    x1s, y1s, z1s = swap(x1, y1, z1)
    carry = call(own_kernel, ids, docs, queries, (), [keys, values], rows)
    carry = far(choose_first, devices_first, carry, [mate_k, mate_v, z1s, z1], rows)
    y2, y1, *carry = barrier((y2, y1, *carry))
    x3 = send(y2, "x")
    z2, y1, y2 = barrier((z2, y1, y2))
    side3, up3 = w(odd_y == 0, x1, z2), w(plane == 0, y1, values)
    y3, z3 = send(side3, "y"), send(up3, "z")
    x2s, y2s, z2s = swap(x2, y2, z2)
    carry = far(choose_middle, functools.partial(devices_middle, False), carry, [x1, y1, x2, y2, z2], 2 * rows)
    x2s, y2s, z2s, *carry = barrier((x2s, y2s, z2s, *carry))
    carry = far(choose_middle, functools.partial(devices_middle, True), carry, [x1s, y1s, x2s, y2s, z2s], 2 * rows)
    x3, y3, z3, *carry = barrier((x3, y3, z3, *carry))
    x3s, y3s, z3s = swap(x3, y3, z3)
    carry = far(choose_last, functools.partial(devices_last, False), carry, [z1, y2, x3, y3, z3], 2 * rows)
    (out,) = far(
        choose_last, functools.partial(devices_last, True), carry, [z1s, y2s, x3s, y3s, z3s], 2 * rows, True
    )
    return out


def solution(mesh):
    split = P(AXES, None)
    return jax.shard_map(
        shards, mesh=mesh, in_specs=(split, split, split, P()), out_specs=split, check_vma=False
    )
```

```python
import functools
import math

import jax
import jax.numpy as jnp
from jax import lax
from jax.experimental import pallas as pl
from jax.experimental.pallas import tpu as pltpu
from jax.sharding import PartitionSpec as P

HEAD_DIM = 128
REACH = 8
AXES = ("section", "attn")
NEG = -1e30
SCALE = HEAD_DIM ** -0.5 * math.log2(math.e)
CHAINS = 2
VMEM_BYTES = 16 * 2**20
HIGH = 2.0 ** 60
barrier = lax.optimization_barrier


def scores(q, k):
    return lax.dot_general(q, k, (((1,), (1,)), ((), ())), preferred_element_type=jnp.float32)


def head_of(array, i):
    return array[:, i * HEAD_DIM:(i + 1) * HEAD_DIM]


def with_ones(v, ok):
    return jnp.concatenate([v * ok, ok], axis=1)


def where_am_i(ids, docs_ref, rows):
    chip, core = ids[0], ids[1]
    first = chip * 2 * rows
    head = docs_ref[pl.ds(first // HEAD_DIM, 1), :][:, :1]
    return chip, core, first, head, jnp.sum((docs_ref[...] < head).astype(jnp.int32))


def units(group, heads):
    for h in range(heads):
        for i in range(h * group, (h + 1) * group):
            for half in range(2):
                yield 2 * i + half, h, i, half


def own_kernel(group, ids, docs_ref, qa_ref, qb_ref, k_ref, v_ref, acc_ref, top_ref, total_ref):
    rows = qa_ref.shape[0]
    _, core, first, head, _ = where_am_i(ids, docs_ref, rows)
    tiles, starts = [], [first + core * rows, first + (1 - core) * rows]
    for start in starts:
        tiles += [docs_ref[pl.ds(start // HEAD_DIM + i, 1), :] for i in range(rows // HEAD_DIM)]
    across = jnp.concatenate(tiles, axis=1)
    down = jnp.concatenate([jnp.broadcast_to(t, (HEAD_DIM, HEAD_DIM)).T for t in tiles], axis=0)
    key = lax.broadcasted_iota(jnp.int32, (rows, 2 * rows), 1)
    key = jnp.where(key < rows, key + starts[0], key + (starts[1] - rows))
    row = lax.broadcasted_iota(jnp.int32, (rows, 2 * rows), 0)
    bias, sees_earlier = [], []
    for half in range(2):
        mine = down[half * rows:(half + 1) * rows]
        same = jnp.concatenate([mine] * (2 * rows // HEAD_DIM), axis=1) == across
        bias.append(jnp.where(same & (key <= row + starts[half]), 0.0, NEG))
        sees_earlier.append(mine == head)
    qs, k, v = (qa_ref[...], qb_ref[...]), k_ref[...], v_ref[...]
    for u, h, i, half in units(group, k.shape[1] // HEAD_DIM):
        s = scores(head_of(qs[half], i), head_of(k, h)) + bias[half]
        top = jnp.max(s, axis=1, keepdims=True)
        w = jnp.exp2((s - top) * SCALE).astype(jnp.bfloat16)
        values = head_of(v, h)
        both = jnp.dot(w, with_ones(values, jnp.ones_like(values)), preferred_element_type=jnp.float32)
        acc_ref[u] = both[:, :HEAD_DIM]
        total_ref[u] = both[:, HEAD_DIM:]
        top_ref[u] = jnp.where(sees_earlier[half], jnp.broadcast_to(top, (rows, HEAD_DIM)), -NEG)


def far_kernel(choose, devices, last, group, ids, docs_ref, qa_ref, qb_ref, acc_in, top_in, total_in, *refs):
    rows = qa_ref.shape[0]
    chip, core, first, _, start = where_am_i(ids, docs_ref, rows)
    plane = chip % 4
    refs, outs = (refs[:-2], refs[-2:]) if last else (refs[:-3], refs[-3:])
    places = [jnp.where((d >= 0) & (d < 2 * chip), d * rows, -(2**30)) for d in devices(plane, core, 2 * chip)]
    needed = functools.reduce(jnp.maximum, places) + rows > start
    heads = refs[0].shape[1] // HEAD_DIM

    def put(u, i, half, total, out, top=None):
        if last:
            outs[half][:, i * HEAD_DIM:(i + 1) * HEAD_DIM] = (out / total).astype(jnp.bfloat16)
            return
        outs[0][u] = out
        if top is not None:
            outs[1][u] = top
        outs[2][u] = total

    def attend(exact):
        at = lax.broadcasted_iota(jnp.int32, (rows, HEAD_DIM), 0)
        ok = [jnp.where(at + place >= start, 1.0, 0.0).astype(jnp.bfloat16) for place in places]
        qs, tiles, high, ready = (qa_ref[...], qb_ref[...]), [r[...] for r in refs], None, -1
        for u, h, i, half in units(group, heads):
            if h != ready:
                ks, vs = choose(plane, [head_of(t, h) for t in tiles])
                k = jnp.concatenate(ks, axis=0)
                v = jnp.concatenate(vs, axis=0)
                v = jnp.concatenate([v * jnp.concatenate(ok, axis=0), jnp.concatenate(ok, axis=0)], axis=1)
                ready = h
            s = scores(head_of(qs[half], i), k)
            top, total, before = top_in[u], total_in[u], acc_in[u]
            if exact:
                key = lax.broadcasted_iota(jnp.int32, (rows, rows), 1)
                allowed = jnp.concatenate([key + place >= start for place in places], axis=1)
                s = jnp.where(allowed, s, NEG)
                new = jnp.maximum(top, jnp.max(s, axis=1, keepdims=True))
                back = jnp.exp2((top - new) * SCALE)
                top, total, before = new, total * back, before * back
            w = []
            for n in range(k.shape[0] // HEAD_DIM):
                part = jnp.exp2((head_of(s, n) - top) * SCALE).astype(jnp.bfloat16)
                w.append(part)
                if not exact:
                    high = part if high is None else jnp.maximum(high, part)
            both = jnp.dot(jnp.concatenate(w, axis=1), v, preferred_element_type=jnp.float32)
            put(u, i, half, total + both[:, HEAD_DIM:], both[:, :HEAD_DIM] + before, top if exact else None)
        return high

    @pl.when(needed)
    def _():
        high = attend(False)

        @pl.when(jnp.max(high.astype(jnp.float32)) > HIGH)
        def _():
            attend(True)

    @pl.when(jnp.logical_not(needed))
    def _():
        for u, _, i, half in units(group, heads):
            put(u, i, half, total_in[u], acc_in[u])


def pick(plane, at0, at1, at2, at3):
    return jnp.where(plane == 0, at0, jnp.where(plane == 1, at1, jnp.where(plane == 2, at2, at3)))


def choose_middle(plane, tiles):
    x1, y1, z1, x2, y2, z2 = tiles
    rows = z1.shape[0] // 2
    odd_v = jnp.concatenate([z1[rows:], z1[rows:]], axis=0)
    pk, pv = pick(plane, x2, x2, y2, x2), pick(plane, z2, x1, y1, x1)
    qk, qv = pick(plane, z1, y2, x2, y2), pick(plane, odd_v, z2, z2, y1)
    return (pk, qk), (pv, qv)


def devices_middle(plane, core, base):
    p = base - 2 * pick(plane, 3, 1, 2, 1)
    q = base - 2 * pick(plane, 0, 2, 3, 2)
    qs = jnp.where(plane == 0, base - 7, q + core), jnp.where(plane == 0, -1, q + 1 - core)
    return (p + core, p + 1 - core, *qs)


def choose_last(plane, tiles):
    z1, y2, x3, y3, z3 = tiles
    pk, pv = pick(plane, y2, x3, x3, x3), pick(plane, z3, y3, y3, y3)
    qk, qv = pick(plane, x3, z1, z1, z1), pick(plane, y3, z3, z3, z3)
    return (pk, qk), (pv, qv)


def devices_last(plane, core, base):
    p, q = base - 2 * pick(plane, 2, 3, 1, 3), base - 2 * pick(plane, 1, 4, 4, 4)
    return p + core, p + 1 - core, q + core, q + 1 - core


def call(kernel, ids, docs, qs, carry, pieces, keys, last=False):
    rows, width = qs[0].shape
    vmem = pl.BlockSpec(memory_space=pltpu.VMEM)
    arrays = [docs, *qs, *carry, *pieces]
    if last:
        out_shape = [jax.ShapeDtypeStruct((rows, width), jnp.bfloat16)] * 2
    else:
        out_shape = [jax.ShapeDtypeStruct((2 * width // HEAD_DIM, rows, HEAD_DIM), jnp.float32)] * 3
    return pl.pallas_call(
        functools.partial(kernel, width // pieces[0].shape[1]),
        in_specs=[pl.BlockSpec(memory_space=pltpu.SMEM)] + [vmem] * len(arrays),
        out_specs=[vmem] * len(out_shape),
        out_shape=out_shape,
        input_output_aliases={5: 1} if carry and not last else {},
        cost_estimate=pl.CostEstimate(
            flops=16 * rows * keys * width, bytes_accessed=4 * rows * width, transcendentals=0
        ),
        compiler_params=pltpu.CompilerParams(vmem_limit_bytes=VMEM_BYTES),
    )(ids, *arrays)


def store_kernel(ids, *refs):
    out, sems = refs[-2:]
    parts = refs[:-2]
    count, width = len(parts) // 2, parts[0].shape[1]
    copies = []
    for n, part in enumerate(parts):
        core = ids[1] if n < count else 1 - ids[1]
        at = pl.multiple_of((core * count + n % count) * width, HEAD_DIM)
        copies.append(pltpu.make_async_copy(part, out.at[:, pl.ds(at, width)], sems.at[n]))
    for copy in copies:
        copy.start()
    for copy in copies:
        copy.wait()


def store(ids, parts):
    rows, width = parts[0].shape
    return pl.pallas_call(
        store_kernel,
        in_specs=[pl.BlockSpec(memory_space=pltpu.SMEM)] + [pl.BlockSpec(memory_space=pltpu.VMEM)] * len(parts),
        out_specs=pl.BlockSpec(memory_space=pl.ANY),
        out_shape=jax.ShapeDtypeStruct((rows, width * len(parts)), parts[0].dtype),
        scratch_shapes=[pltpu.SemaphoreType.DMA((len(parts),))],
        compiler_params=pltpu.CompilerParams(vmem_limit_bytes=VMEM_BYTES),
    )(ids, *parts)


def shards(queries, keys, values, doc_ids):
    rows = queries.shape[0]
    chips, cores = lax.axis_size("section"), lax.axis_size("attn")
    chip, core = lax.axis_index("section"), lax.axis_index("attn")
    plane, odd_x, odd_y = chip % 4, chip % 2, (chip // 2) % 2
    w = jnp.where

    def routes(target):
        return [
            (c * cores + k, at * cores + to)
            for c in range(chips) for k in range(cores) for at, to in [target(c, k)]
        ]

    along = {
        "x": routes(lambda c, k: (c ^ 1, k)),
        "y": routes(lambda c, k: (c ^ 2, k)),
        "z": routes(lambda c, k: ((c + 4) % chips, k)),
        "mate": routes(lambda c, k: (c, 1 - k)),
    }

    def send(array, way):
        return lax.ppermute(array, AXES, along[way])

    ids = jnp.stack([chip, core])
    docs = doc_ids.reshape(-1, HEAD_DIM)

    def halves(array):
        mid = array.shape[1] // 2
        low, high = array[:, :mid], array[:, mid:]
        return w(core == 0, low, high), w(core == 0, high, low)

    def chained(array, a):
        width = array.shape[1] // CHAINS
        return array[:, a * width:(a + 1) * width]

    def far(choose, devices, a, carry, pieces, last=False):
        kernel = functools.partial(far_kernel, choose, devices, last)
        return call(kernel, ids, docs, qs[a], carry, pieces, 4 * rows, last)

    (my_k, their_k), (my_v, their_v) = halves(keys), halves(values)
    mate_k, mate_v = send(their_k, "mate"), send(their_v, "mate")
    my_q, their_q = halves(queries)
    mate_q = send(their_q, "mate")
    qs = [(chained(my_q, a), chained(mate_q, a)) for a in range(CHAINS)]
    k, v, first = [], [], []
    for a in range(CHAINS):
        k.append(jnp.concatenate([chained(my_k, a), chained(mate_k, a)], axis=0))
        v.append(jnp.concatenate([chained(my_v, a), chained(mate_v, a)], axis=0))
        odd = [w(core == 1, chained(m, a), chained(t, a)) for m, t in ((my_k, mate_k), (my_v, mate_v))]
        first.append(w(plane == 0, jnp.concatenate(odd, axis=0), k[a]))
    k, v, first = [list(t) for t in barrier((tuple(k), tuple(v), tuple(first)))]

    def round1(a):
        return send(first[a], "z"), send(v[a], "x"), send(v[a], "y")

    def round2(a, z1, x1, y1):
        return (
            send(w(odd_x == 0, k[a], z1), "x"), send(w(odd_y == 0, k[a], z1), "y"), send(w(plane == 1, y1, x1), "z")
        )

    def round3(a, x1, y1, x2, y2, z2):
        return send(y2, "x"), send(w(odd_y == 0, x1, z2), "y"), send(w(plane == 0, y1, v[a]), "z")

    def own(a):
        return call(own_kernel, ids, docs, qs[a], (), [k[a], v[a]], 2 * rows)

    a, b = 0, 1
    a1, b1 = round1(a), round1(b)
    carry_a = own(a)
    a1, carry_a = barrier((a1, carry_a))
    a2 = round2(a, *a1)
    carry_b = own(b)
    b1, carry_b = barrier((b1, carry_b))
    b2 = round2(b, *b1)
    a2 = barrier(a2)
    a3 = round3(a, a1[1], a1[2], *a2)
    (z1, x1, y1), (x2, y2, z2) = a1, a2
    carry_a = far(choose_middle, devices_middle, a, carry_a, [x1, y1, z1, x2, y2, z2])
    b2, carry_a = barrier((b2, carry_a))
    b3 = round3(b, b1[1], b1[2], *b2)
    (z1, x1, y1), (x2, y2, z2) = b1, b2
    carry_b = far(choose_middle, devices_middle, b, carry_b, [x1, y1, z1, x2, y2, z2])
    a3, carry_b = barrier((a3, carry_b))
    (x3, y3, z3) = a3
    mine_a, theirs_a = far(choose_last, devices_last, a, carry_a, [a1[0], a2[1], x3, y3, z3], True)
    b3, mine_a, theirs_a = barrier((b3, mine_a, theirs_a))
    back_a = send(theirs_a, "mate")
    (x3, y3, z3) = b3
    mine_b, theirs_b = far(choose_last, devices_last, b, carry_b, [b1[0], b2[1], x3, y3, z3], True)
    back_b = send(theirs_b, "mate")
    return store(ids, [mine_a, mine_b, back_a, back_b])


def solution(mesh):
    split = P(AXES, None)
    return jax.shard_map(
        shards, mesh=mesh, in_specs=(split, split, split, P()), out_specs=split, check_vma=False
    )
```

```python
import functools
import math

import jax
import jax.numpy as jnp
from jax import lax
from jax.experimental import pallas as pl
from jax.experimental.pallas import tpu as pltpu
from jax.sharding import PartitionSpec as P

HEAD_DIM = 128
REACH = 8
AXES = ("section", "attn")
NEG = -1e30
SCALE = HEAD_DIM ** -0.5 * math.log2(math.e)
HEADS_STEP = 4
VMEM_BYTES = 16 * 2**20
HIGH = 2.0 ** 60
barrier = lax.optimization_barrier


def scores(q, k):
    return lax.dot_general(q, k, (((1,), (1,)), ((), ())), preferred_element_type=jnp.float32)


def heads_of(ref, step, count):
    at = pl.multiple_of(step * (count * HEAD_DIM), HEAD_DIM)
    return [ref[:, pl.ds(at + i * HEAD_DIM, HEAD_DIM)] for i in range(count)]


def put_head(ref, step, count, i, value):
    at = pl.multiple_of(step * (count * HEAD_DIM), HEAD_DIM)
    ref[:, pl.ds(at + i * HEAD_DIM, HEAD_DIM)] = value


def with_ones(v, ok):
    return jnp.concatenate([v * ok, ok], axis=1)


def where_am_i(ids, docs_ref, rows):
    chip, core = ids[0], ids[1]
    first = (chip * ids[2] + core) * rows
    head = docs_ref[pl.ds(first // HEAD_DIM, 1), :][:, :1]
    earlier = (docs_ref[...] < head).astype(jnp.int32)
    return chip, core, first, jnp.sum(earlier), head


def own_kernel(group, ids, docs_ref, q_ref, k_ref, v_ref, acc_ref, top_ref, total_ref):
    rows = q_ref.shape[0]
    count = HEADS_STEP * group
    _, _, first, _, head = where_am_i(ids, docs_ref, rows)
    tiles = [docs_ref[pl.ds(first // HEAD_DIM + i, 1), :] for i in range(rows // HEAD_DIM)]
    across = jnp.concatenate(tiles, axis=1)
    down = jnp.concatenate([jnp.broadcast_to(t, (HEAD_DIM, HEAD_DIM)).T for t in tiles], axis=0)
    same = jnp.concatenate([down] * (rows // HEAD_DIM), axis=1) == across
    at = lax.broadcasted_iota(jnp.int32, (rows, rows), 1)
    row = lax.broadcasted_iota(jnp.int32, (rows, rows), 0)
    bias = jnp.where(same & (at <= row), 0.0, NEG)
    sees_earlier = down == head

    def step(j, _):
        qs = heads_of(q_ref, j, count)
        ks, vs = heads_of(k_ref, j, HEADS_STEP), heads_of(v_ref, j, HEADS_STEP)
        for i in range(count):
            s = scores(qs[i], ks[i // group]) + bias
            top = jnp.max(s, axis=1, keepdims=True)
            w = jnp.exp2((s - top) * SCALE).astype(jnp.bfloat16)
            v = vs[i // group]
            both = jnp.dot(w, with_ones(v, jnp.ones_like(v)), preferred_element_type=jnp.float32)
            put_head(acc_ref, j, count, i, both[:, :HEAD_DIM])
            total_ref[j * count + i] = both[:, HEAD_DIM:]
            top_ref[j * count + i] = jnp.where(sees_earlier, jnp.broadcast_to(top, (rows, HEAD_DIM)), -NEG)
        return 0

    lax.fori_loop(0, k_ref.shape[1] // HEAD_DIM // HEADS_STEP, step, 0)


def far_kernel(choose, devices, last, group, ids, docs_ref, q_ref, acc_in, top_in, total_in, *refs):
    rows = q_ref.shape[0]
    chip, core, first, start, _ = where_am_i(ids, docs_ref, rows)
    plane, owner = chip % 4, first // rows
    places = [jnp.where((d >= 0) & (d < owner), d * rows, -(2**30)) for d in devices(plane, core, chip * ids[2])]
    if last:
        refs, (hbm, acc_out, sems) = refs[:-3], refs[-3:]
    else:
        refs, (acc_out, top_out, total_out) = refs[:-3], refs[-3:]
    count = HEADS_STEP * group
    steps = refs[0].shape[1] // HEAD_DIM // HEADS_STEP
    needed = functools.reduce(jnp.maximum, places) + rows > start

    def put(j, i, total, out, top=None):
        if last:
            out = (out / total).astype(jnp.bfloat16)
        else:
            if top is not None:
                top_out[j * count + i] = top
            total_out[j * count + i] = total
        put_head(acc_out, j, count, i, out)

    def attend(j, exact):
        qs, befores = heads_of(q_ref, j, count), heads_of(acc_in, j, count)
        tiles = [heads_of(r, j, HEADS_STEP) for r in refs]
        at = lax.broadcasted_iota(jnp.int32, (rows, HEAD_DIM), 0)
        high = None
        for h in range(HEADS_STEP):
            ks, vs = choose(plane, core, [t[h] for t in tiles])
            k = jnp.concatenate(ks, axis=0)
            ok = [jnp.where(at + place >= start, 1.0, 0.0).astype(jnp.bfloat16) for place in places]
            v = jnp.concatenate([with_ones(v, o) for v, o in zip(vs, ok)], axis=0)
            for i in range(h * group, (h + 1) * group):
                s = scores(qs[i], k)
                top, total, before = top_in[j * count + i], total_in[j * count + i], befores[i]
                if exact:
                    key = lax.broadcasted_iota(jnp.int32, (rows, rows), 1)
                    allowed = jnp.concatenate([key + place >= start for place in places], axis=1)
                    s = jnp.where(allowed, s, NEG)
                    new = jnp.maximum(top, jnp.max(s, axis=1, keepdims=True))
                    back = jnp.exp2((top - new) * SCALE)
                    top, total, before = new, total * back, before * back
                w = []
                for n in range(k.shape[0] // HEAD_DIM):
                    part = jnp.exp2((s[:, n * HEAD_DIM:(n + 1) * HEAD_DIM] - top) * SCALE).astype(jnp.bfloat16)
                    w.append(part)
                    if not exact:
                        high = part if high is None else jnp.maximum(high, part)
                both = jnp.dot(jnp.concatenate(w, axis=1), v, preferred_element_type=jnp.float32)
                put(j, i, total + both[:, HEAD_DIM:], both[:, :HEAD_DIM] + before, top if exact else None)
        return high

    def step(j, _):
        @pl.when(needed)
        def _():
            high = attend(j, False)

            @pl.when(jnp.max(high.astype(jnp.float32)) > HIGH)
            def _():
                attend(j, True)

        @pl.when(jnp.logical_not(needed))
        def _():
            for i, before in enumerate(heads_of(acc_in, j, count)):
                put(j, i, total_in[j * count + i], before)

        if last:
            part(j).start()
        return 0

    def part(j):
        width = count * HEAD_DIM
        columns = pl.ds(pl.multiple_of(j * width, width), width)
        return pltpu.make_async_copy(acc_out.at[:, columns], hbm.at[:, columns], sems.at[j])

    lax.fori_loop(0, steps, step, 0)
    if last:
        for j in range(steps):
            part(j).wait()


def pick(plane, at0, at1, at2, at3):
    return jnp.where(plane == 0, at0, jnp.where(plane == 1, at1, jnp.where(plane == 2, at2, at3)))


def choose_first(plane, core, tiles):
    return tiles[:1], tiles[1:]


def devices_first(plane, core, base):
    return (jnp.where(core == 1, base, jnp.where(plane == 0, base - 7, -1)),)


def choose_middle(plane, core, tiles):
    x1, y1, x2, y2, z2 = tiles
    pk, pv = pick(plane, x2, x2, y2, x2), pick(plane, z2, x1, y1, x1)
    qk, qv = pick(plane, y2, y2, x2, y2), pick(plane, z2, z2, z2, y1)
    return (pk, qk), (pv, qv)


def devices_middle(mates, plane, core, base):
    part = 1 - core if mates else core
    return base - 2 * pick(plane, 3, 1, 2, 1) + part, pick(plane, -8, base - 4, base - 6, base - 4) + part


def choose_last(plane, core, tiles):
    z1, y2, x3, y3, z3 = tiles
    pk, pv = pick(plane, y2, x3, x3, x3), pick(plane, z3, y3, y3, y3)
    qk, qv = pick(plane, x3, z1, z1, z1), pick(plane, y3, z3, z3, z3)
    return (pk, qk), (pv, qv)


def devices_last(mates, plane, core, base):
    part = 1 - core if mates else core
    return base - 2 * pick(plane, 2, 3, 1, 3) + part, base - 2 * pick(plane, 1, 4, 4, 4) + part


def call(kernel, ids, docs, q, carry, pieces, keys, last=False):
    rows, width = q.shape
    steps = pieces[0].shape[1] // HEAD_DIM // HEADS_STEP
    group = width // pieces[0].shape[1]
    vmem = pl.BlockSpec(memory_space=pltpu.VMEM)
    arrays = [docs, q, *carry, *pieces]
    if last:
        out_shape = [jax.ShapeDtypeStruct(q.shape, jnp.bfloat16)]
        scratch = [pltpu.VMEM(q.shape, jnp.bfloat16), pltpu.SemaphoreType.DMA((steps,))]
    else:
        out_shape = [jax.ShapeDtypeStruct(q.shape, jnp.float32)]
        out_shape += [jax.ShapeDtypeStruct((width // HEAD_DIM, rows, HEAD_DIM), jnp.float32)] * 2
        scratch = []
    return pl.pallas_call(
        functools.partial(kernel, group),
        in_specs=[pl.BlockSpec(memory_space=pltpu.SMEM)] + [vmem] * len(arrays),
        out_specs=[pl.BlockSpec(memory_space=pl.ANY) if last else vmem] * len(out_shape),
        out_shape=out_shape,
        scratch_shapes=scratch,
        input_output_aliases={4: 1} if carry and not last else {},
        cost_estimate=pl.CostEstimate(
            flops=8 * rows * keys * width, bytes_accessed=4 * rows * width, transcendentals=0
        ),
        compiler_params=pltpu.CompilerParams(vmem_limit_bytes=VMEM_BYTES),
    )(ids, *arrays)


def shards(queries, keys, values, doc_ids):
    rows = queries.shape[0]
    chips, cores = lax.axis_size("section"), lax.axis_size("attn")
    chip, core = lax.axis_index("section"), lax.axis_index("attn")
    plane, odd_x, odd_y = chip % 4, chip % 2, (chip // 2) % 2

    def routes(target):
        return [
            (c * cores + k, at * cores + to)
            for c in range(chips) for k in range(cores) for at, to in [target(c, k)]
        ]

    along = {
        "x": routes(lambda c, k: (c ^ 1, k)),
        "y": routes(lambda c, k: (c ^ 2, k)),
        "z": routes(lambda c, k: ((c + 4) % chips, k)),
        "mate": routes(lambda c, k: (c, 1 - k)),
        "first_z": routes(lambda c, k: ((c + 4) % chips, k) if c % 4 else (c, 1 - k)),
        "first_mate": routes(lambda c, k: ((c + 4) % chips, 0) if c % 4 == 0 and k else (c, 1 - k)),
    }

    def send(array, way):
        return lax.ppermute(array, AXES, along[way])

    def swap(*arrays):
        return tuple(send(a, "mate") for a in arrays)

    ids = jnp.stack([chip, core, jnp.int32(cores)])
    docs = doc_ids.reshape(-1, HEAD_DIM)
    w = jnp.where

    def far(choose, devices, carry, pieces, keys, last=False):
        kernel = functools.partial(far_kernel, choose, devices, last)
        return call(kernel, ids, docs, queries, carry, pieces, keys, last)

    z1 = send(keys, "first_z")
    x1, y1 = send(values, "x"), send(values, "y")
    mate_k, mate_v = send(keys, "first_mate"), send(values, "first_mate")
    z1, mate_k, mate_v = barrier((z1, mate_k, mate_v))
    across2, side2 = w(odd_x == 0, keys, z1), w(odd_y == 0, keys, z1)
    x2, y2 = send(across2, "x"), send(side2, "y")
    x1, y1, _, _ = barrier((x1, y1, across2, side2))
    z2 = send(w(plane == 1, y1, x1), "z")
    x1s, y1s = swap(x1, y1)
    carry = call(own_kernel, ids, docs, queries, (), [keys, values], rows)
    carry = far(choose_first, devices_first, carry, [mate_k, mate_v], rows)
    y2, z2, y1, x1s, y1s, *carry = barrier((y2, z2, y1, x1s, y1s, *carry))
    x3 = send(y2, "x")
    side3, up3 = w(odd_y == 0, x1, z2), w(plane == 0, y1, values)
    y3, z3 = send(side3, "y"), send(up3, "z")
    x2s, y2s, z2s = swap(x2, y2, z2)
    carry = far(choose_middle, functools.partial(devices_middle, False), carry, [x1, y1, x2, y2, z2], 2 * rows)
    x2s, y2s, z2s, *carry = barrier((x2s, y2s, z2s, *carry))
    carry = far(choose_middle, functools.partial(devices_middle, True), carry, [x1s, y1s, x2s, y2s, z2s], 2 * rows)
    x3, y3, z3, *carry = barrier((x3, y3, z3, *carry))
    z1s, x3s, y3s, z3s = swap(z1, x3, y3, z3)
    carry = far(choose_last, functools.partial(devices_last, False), carry, [z1, y2, x3, y3, z3], 2 * rows)
    (out,) = far(
        choose_last, functools.partial(devices_last, True), carry, [z1s, y2s, x3s, y3s, z3s], 2 * rows, True
    )
    return out


def solution(mesh):
    split = P(AXES, None)
    return jax.shard_map(
        shards, mesh=mesh, in_specs=(split, split, split, P()), out_specs=split, check_vma=False
    )
```

```python
import functools
import math

import jax
import jax.numpy as jnp
from jax import lax
from jax.experimental import pallas as pl
from jax.experimental.pallas import tpu as pltpu
from jax.sharding import PartitionSpec as P

HEAD_DIM = 128
REACH = 8
AXES = ("section", "attn")
NEG = -1e30
SCALE = HEAD_DIM ** -0.5 * math.log2(math.e)
HEADS_STEP = 4
VMEM_BYTES = 8 * 2**20
HIGH = 2.0 ** 60
barrier = lax.optimization_barrier


def scores(q, k):
    return lax.dot_general(q, k, (((1,), (1,)), ((), ())), preferred_element_type=jnp.float32)


def heads_of(ref, step, count):
    at = pl.multiple_of(step * (count * HEAD_DIM), HEAD_DIM)
    return [ref[:, pl.ds(at + i * HEAD_DIM, HEAD_DIM)] for i in range(count)]


def put_head(ref, step, count, i, value):
    at = pl.multiple_of(step * (count * HEAD_DIM), HEAD_DIM)
    ref[:, pl.ds(at + i * HEAD_DIM, HEAD_DIM)] = value


def with_ones(v, ok):
    return jnp.concatenate([v * ok, ok], axis=1)


def where_am_i(ids, docs_ref, rows):
    chip, core = ids[0], ids[1]
    first = (chip * ids[2] + core) * rows
    head = docs_ref[pl.ds(first // HEAD_DIM, 1), :][:, :1]
    earlier = (docs_ref[...] < head).astype(jnp.int32)
    return chip, core, first, jnp.sum(earlier), head


def own_kernel(group, ids, docs_ref, q_ref, k_ref, v_ref, acc_ref, top_ref, total_ref):
    rows = q_ref.shape[0]
    count = HEADS_STEP * group
    _, _, first, _, head = where_am_i(ids, docs_ref, rows)
    tiles = [docs_ref[pl.ds(first // HEAD_DIM + i, 1), :] for i in range(rows // HEAD_DIM)]
    across = jnp.concatenate(tiles, axis=1)
    down = jnp.concatenate([jnp.broadcast_to(t, (HEAD_DIM, HEAD_DIM)).T for t in tiles], axis=0)
    same = jnp.concatenate([down] * (rows // HEAD_DIM), axis=1) == across
    at = lax.broadcasted_iota(jnp.int32, (rows, rows), 1)
    row = lax.broadcasted_iota(jnp.int32, (rows, rows), 0)
    bias = jnp.where(same & (at <= row), 0.0, NEG)
    sees_earlier = down == head

    def step(j, _):
        qs = heads_of(q_ref, j, count)
        ks, vs = heads_of(k_ref, j, HEADS_STEP), heads_of(v_ref, j, HEADS_STEP)
        for i in range(count):
            s = scores(qs[i], ks[i // group]) + bias
            top = jnp.max(s, axis=1, keepdims=True)
            w = jnp.exp2((s - top) * SCALE).astype(jnp.bfloat16)
            v = vs[i // group]
            both = jnp.dot(w, with_ones(v, jnp.ones_like(v)), preferred_element_type=jnp.float32)
            put_head(acc_ref, j, count, i, both[:, :HEAD_DIM])
            total_ref[j * count + i] = both[:, HEAD_DIM:]
            top_ref[j * count + i] = jnp.where(sees_earlier, jnp.broadcast_to(top, (rows, HEAD_DIM)), -NEG)
        return 0

    lax.fori_loop(0, k_ref.shape[1] // HEAD_DIM // HEADS_STEP, step, 0)


def far_kernel(choose, devices, last, group, ids, docs_ref, q_ref, acc_in, top_in, total_in, *refs):
    rows = q_ref.shape[0]
    chip, core, first, start, _ = where_am_i(ids, docs_ref, rows)
    plane, owner = chip % 4, first // rows
    places = [jnp.where((d >= 0) & (d < owner), d * rows, -(2**30)) for d in devices(plane, core, chip * ids[2])]
    if last:
        refs, (hbm, acc_out, sems) = refs[:-3], refs[-3:]
    else:
        refs, (acc_out, top_out, total_out) = refs[:-3], refs[-3:]
    count = HEADS_STEP * group
    steps = refs[0].shape[1] // HEAD_DIM // HEADS_STEP
    needed = functools.reduce(jnp.maximum, places) + rows > start

    def put(j, i, total, out, top=None):
        if last:
            out = (out / total).astype(jnp.bfloat16)
        else:
            if top is not None:
                top_out[j * count + i] = top
            total_out[j * count + i] = total
        put_head(acc_out, j, count, i, out)

    def attend(j, exact):
        qs, befores = heads_of(q_ref, j, count), heads_of(acc_in, j, count)
        tiles = [heads_of(r, j, HEADS_STEP) for r in refs]
        at = lax.broadcasted_iota(jnp.int32, (rows, HEAD_DIM), 0)
        high = None
        for h in range(HEADS_STEP):
            ks, vs = choose(plane, core, [t[h] for t in tiles])
            k = jnp.concatenate(ks, axis=0)
            ok = [jnp.where(at + place >= start, 1.0, 0.0).astype(jnp.bfloat16) for place in places]
            v = jnp.concatenate([with_ones(v, o) for v, o in zip(vs, ok)], axis=0)
            members = range(h * group, (h + 1) * group)
            s_all = scores(jnp.concatenate([qs[i] for i in members], axis=0), k)
            sums, w_all = [], []
            for n, i in enumerate(members):
                s = s_all[n * rows:(n + 1) * rows]
                top, total, before = top_in[j * count + i], total_in[j * count + i], befores[i]
                if exact:
                    key = lax.broadcasted_iota(jnp.int32, (rows, rows), 1)
                    allowed = jnp.concatenate([key + place >= start for place in places], axis=1)
                    s = jnp.where(allowed, s, NEG)
                    new = jnp.maximum(top, jnp.max(s, axis=1, keepdims=True))
                    back = jnp.exp2((top - new) * SCALE)
                    top, total, before = new, total * back, before * back
                w = []
                for m in range(k.shape[0] // HEAD_DIM):
                    part = jnp.exp2((s[:, m * HEAD_DIM:(m + 1) * HEAD_DIM] - top) * SCALE).astype(jnp.bfloat16)
                    w.append(part)
                    if not exact:
                        high = part if high is None else jnp.maximum(high, part)
                w_all.append(jnp.concatenate(w, axis=1))
                sums.append((top if exact else None, total, before))
            both_all = jnp.dot(jnp.concatenate(w_all, axis=0), v, preferred_element_type=jnp.float32)
            for n, i in enumerate(members):
                both = both_all[n * rows:(n + 1) * rows]
                top, total, before = sums[n]
                put(j, i, total + both[:, HEAD_DIM:], both[:, :HEAD_DIM] + before, top)
        return high

    def step(j, _):
        @pl.when(needed)
        def _():
            high = attend(j, False)

            @pl.when(jnp.max(high.astype(jnp.float32)) > HIGH)
            def _():
                attend(j, True)

        @pl.when(jnp.logical_not(needed))
        def _():
            for i, before in enumerate(heads_of(acc_in, j, count)):
                put(j, i, total_in[j * count + i], before)

        if last:
            part(j).start()
        return 0

    def part(j):
        width = count * HEAD_DIM
        columns = pl.ds(pl.multiple_of(j * width, width), width)
        return pltpu.make_async_copy(acc_out.at[:, columns], hbm.at[:, columns], sems.at[j])

    lax.fori_loop(0, steps, step, 0)
    if last:
        for j in range(steps):
            part(j).wait()


def pick(plane, at0, at1, at2, at3):
    return jnp.where(plane == 0, at0, jnp.where(plane == 1, at1, jnp.where(plane == 2, at2, at3)))


def choose_first(plane, core, tiles):
    return tiles[:1], tiles[1:]


def devices_first(plane, core, base):
    return (jnp.where(core == 1, base, jnp.where(plane == 0, base - 7, -1)),)


def choose_middle(plane, core, tiles):
    def half(x1, y1, x2, y2, z2):
        pk, pv = pick(plane, x2, x2, y2, x2), pick(plane, z2, x1, y1, x1)
        qk, qv = pick(plane, y2, y2, x2, y2), pick(plane, z2, z2, z2, y1)
        return (pk, qk), (pv, qv)
    a, b = half(*tiles[:5]), half(*tiles[5:])
    return a[0] + b[0], a[1] + b[1]


def devices_middle(plane, core, base):
    p = base - 2 * pick(plane, 3, 1, 2, 1)
    q = pick(plane, -8, base - 4, base - 6, base - 4)
    return p + core, q + core, p + 1 - core, q + 1 - core


def choose_last(plane, core, tiles):
    z1, y2, x3, y3, z3 = tiles
    pk, pv = pick(plane, y2, x3, x3, x3), pick(plane, z3, y3, y3, y3)
    qk, qv = pick(plane, x3, z1, z1, z1), pick(plane, y3, z3, z3, z3)
    return (pk, qk), (pv, qv)


def devices_last(mates, plane, core, base):
    part = 1 - core if mates else core
    return base - 2 * pick(plane, 2, 3, 1, 3) + part, base - 2 * pick(plane, 1, 4, 4, 4) + part


def call(kernel, ids, docs, q, carry, pieces, keys, last=False):
    rows, width = q.shape
    steps = pieces[0].shape[1] // HEAD_DIM // HEADS_STEP
    group = width // pieces[0].shape[1]
    vmem = pl.BlockSpec(memory_space=pltpu.VMEM)
    arrays = [docs, q, *carry, *pieces]
    if last:
        out_shape = [jax.ShapeDtypeStruct(q.shape, jnp.bfloat16)]
        scratch = [pltpu.VMEM(q.shape, jnp.bfloat16), pltpu.SemaphoreType.DMA((steps,))]
    else:
        out_shape = [jax.ShapeDtypeStruct(q.shape, jnp.float32)]
        out_shape += [jax.ShapeDtypeStruct((width // HEAD_DIM, rows, HEAD_DIM), jnp.float32)] * 2
        scratch = []
    return pl.pallas_call(
        functools.partial(kernel, group),
        in_specs=[pl.BlockSpec(memory_space=pltpu.SMEM)] + [vmem] * len(arrays),
        out_specs=[pl.BlockSpec(memory_space=pl.ANY) if last else vmem] * len(out_shape),
        out_shape=out_shape,
        scratch_shapes=scratch,
        input_output_aliases={4: 1} if carry and not last else {},
        cost_estimate=pl.CostEstimate(
            flops=8 * rows * keys * width, bytes_accessed=4 * keys * width, transcendentals=0
        ),
        compiler_params=pltpu.CompilerParams(vmem_limit_bytes=VMEM_BYTES),
    )(ids, *arrays)


def mix_kernel(rule, ids, *refs):
    rule(ids[0] % 4, *refs)


def mix(rule, ids, arrays, count, flops=0):
    vmem = pl.BlockSpec(memory_space=pltpu.VMEM)
    return pl.pallas_call(
        functools.partial(mix_kernel, rule),
        in_specs=[pl.BlockSpec(memory_space=pltpu.SMEM)] + [vmem] * len(arrays),
        out_specs=[vmem] * count,
        out_shape=[jax.ShapeDtypeStruct(arrays[0].shape, arrays[0].dtype)] * count,
        cost_estimate=pl.CostEstimate(flops=flops, bytes_accessed=arrays[0].size, transcendentals=0),
        compiler_params=pltpu.CompilerParams(vmem_limit_bytes=VMEM_BYTES),
    )(ids, *arrays)


def mix_round2(plane, keys, z1, across, side):
    across[...] = jnp.where(plane % 2 == 0, keys[...], z1[...])
    side[...] = jnp.where(plane // 2 == 0, keys[...], z1[...])


def mix_up(plane, x1, y1, up):
    up[...] = jnp.where(plane == 1, y1[...], x1[...])


def mix_round3(plane, x1, z2, y1, values, side, up):
    side[...] = jnp.where(plane // 2 == 0, x1[...], z2[...])
    up[...] = jnp.where(plane == 0, y1[...], values[...])


def shards(queries, keys, values, doc_ids):
    rows = queries.shape[0]
    chips, cores = lax.axis_size("section"), lax.axis_size("attn")
    chip, core = lax.axis_index("section"), lax.axis_index("attn")

    def routes(target):
        return [
            (c * cores + k, at * cores + to)
            for c in range(chips) for k in range(cores) for at, to in [target(c, k)]
        ]

    along = {
        "x": routes(lambda c, k: (c ^ 1, k)),
        "y": routes(lambda c, k: (c ^ 2, k)),
        "z": routes(lambda c, k: ((c + 4) % chips, k)),
        "mate": routes(lambda c, k: (c, 1 - k)),
        "first_z": routes(lambda c, k: ((c + 4) % chips, k) if c % 4 else (c, 1 - k)),
        "first_mate": routes(lambda c, k: ((c + 4) % chips, 0) if c % 4 == 0 and k else (c, 1 - k)),
    }

    def send(array, way):
        return lax.ppermute(array, AXES, along[way])

    def swap(*arrays):
        return tuple(send(a, "mate") for a in arrays)

    ids = jnp.stack([chip, core, jnp.int32(cores)])
    docs = doc_ids.reshape(-1, HEAD_DIM)

    def far(choose, devices, carry, pieces, keys, last=False):
        kernel = functools.partial(far_kernel, choose, devices, last)
        return call(kernel, ids, docs, queries, carry, pieces, keys, last)

    z1 = send(keys, "first_z")
    x1, y1 = send(values, "x"), send(values, "y")
    mate_k, mate_v = send(keys, "first_mate"), send(values, "first_mate")
    carry = call(own_kernel, ids, docs, queries, (), [keys, values], rows)
    z1, mate_k, mate_v, *carry = barrier((z1, mate_k, mate_v, *carry))
    across2, side2 = mix(mix_round2, ids, [keys, z1], 2)
    x2, y2 = send(across2, "x"), send(side2, "y")
    x1, y1, _, _ = barrier((x1, y1, across2, side2))
    (up2,) = mix(mix_up, ids, [x1, y1], 1, 2 * 10**10)
    z2 = send(up2, "z")
    x1s, y1s = swap(x1, y1)
    carry = far(choose_first, devices_first, carry, [mate_k, mate_v], 0)
    y2, z2, y1, x1s, y1s, *carry = barrier((y2, z2, y1, x1s, y1s, *carry))
    x3 = send(y2, "x")
    side3, up3 = mix(mix_round3, ids, [x1, z2, y1, values], 2, 2 * 10**10)
    y3, z3 = send(side3, "y"), send(up3, "z")
    x2s, y2s, z2s = swap(x2, y2, z2)
    carry = far(
        choose_middle, devices_middle, carry, [x1, y1, x2, y2, z2, x1s, y1s, x2s, y2s, z2s], 0
    )
    x3, y3, z3, *carry = barrier((x3, y3, z3, *carry))
    z1s, x3s, y3s, z3s = swap(z1, x3, y3, z3)
    carry = far(choose_last, functools.partial(devices_last, False), carry, [z1, y2, x3, y3, z3], 2 * rows)
    (out,) = far(
        choose_last, functools.partial(devices_last, True), carry, [z1s, y2s, x3s, y3s, z3s], 2 * rows, True
    )
    return out


def solution(mesh):
    split = P(AXES, None)
    return jax.shard_map(
        shards, mesh=mesh, in_specs=(split, split, split, P()), out_specs=split, check_vma=False
    )
```

```python
import functools
import math

import jax
import jax.numpy as jnp
from jax import lax
from jax.experimental import pallas as pl
from jax.experimental.pallas import tpu as pltpu
from jax.sharding import PartitionSpec as P

HEAD_DIM = 128
REACH = 8
AXES = ("section", "attn")
NEG = -1e30
SCALE = HEAD_DIM ** -0.5 * math.log2(math.e)
HEADS_STEP = 4
VMEM_BYTES = 8 * 2**20
HIGH = 2.0 ** 60
barrier = lax.optimization_barrier


def scores(q, k):
    return lax.dot_general(q, k, (((1,), (1,)), ((), ())), preferred_element_type=jnp.float32)


def heads_of(ref, step, count):
    at = pl.multiple_of(step * (count * HEAD_DIM), HEAD_DIM)
    return [ref[:, pl.ds(at + i * HEAD_DIM, HEAD_DIM)] for i in range(count)]


def put_head(ref, step, count, i, value):
    at = pl.multiple_of(step * (count * HEAD_DIM), HEAD_DIM)
    ref[:, pl.ds(at + i * HEAD_DIM, HEAD_DIM)] = value


def with_ones(v, ok):
    return jnp.concatenate([v * ok, ok], axis=1)


def where_am_i(ids, docs_ref, rows):
    chip, core = ids[0], ids[1]
    first = (chip * ids[2] + core) * rows
    head = docs_ref[pl.ds(first // HEAD_DIM, 1), :][:, :1]
    earlier = (docs_ref[...] < head).astype(jnp.int32)
    return chip, core, first, jnp.sum(earlier), head


def own_kernel(group, ids, docs_ref, q_ref, k_ref, v_ref, acc_ref, top_ref, total_ref):
    rows = q_ref.shape[0]
    count = HEADS_STEP * group
    _, _, first, _, head = where_am_i(ids, docs_ref, rows)
    tiles = [docs_ref[pl.ds(first // HEAD_DIM + i, 1), :] for i in range(rows // HEAD_DIM)]
    across = jnp.concatenate(tiles, axis=1)
    down = jnp.concatenate([jnp.broadcast_to(t, (HEAD_DIM, HEAD_DIM)).T for t in tiles], axis=0)
    same = jnp.concatenate([down] * (rows // HEAD_DIM), axis=1) == across
    at = lax.broadcasted_iota(jnp.int32, (rows, rows), 1)
    row = lax.broadcasted_iota(jnp.int32, (rows, rows), 0)
    bias = jnp.where(same & (at <= row), 0.0, NEG)
    sees_earlier = down == head

    def step(j, _):
        qs = heads_of(q_ref, j, count)
        ks, vs = heads_of(k_ref, j, HEADS_STEP), heads_of(v_ref, j, HEADS_STEP)
        for i in range(count):
            s = scores(qs[i], ks[i // group]) + bias
            top = jnp.max(s, axis=1, keepdims=True)
            w = jnp.exp2((s - top) * SCALE).astype(jnp.bfloat16)
            v = vs[i // group]
            both = jnp.dot(w, with_ones(v, jnp.ones_like(v)), preferred_element_type=jnp.float32)
            put_head(acc_ref, j, count, i, both[:, :HEAD_DIM])
            total_ref[j * count + i] = both[:, HEAD_DIM:]
            top_ref[j * count + i] = jnp.where(sees_earlier, jnp.broadcast_to(top, (rows, HEAD_DIM)), -NEG)
        return 0

    lax.fori_loop(0, k_ref.shape[1] // HEAD_DIM // HEADS_STEP, step, 0)


def far_kernel(choose, devices, last, heads_step, group, ids, docs_ref, q_ref, acc_in, top_in, total_in, *refs):
    rows = q_ref.shape[0]
    chip, core, first, start, _ = where_am_i(ids, docs_ref, rows)
    plane, owner = chip % 4, first // rows
    places = [jnp.where((d >= 0) & (d < owner), d * rows, -(2**30)) for d in devices(plane, core, chip * ids[2])]
    if last:
        refs, (hbm, acc_out, sems) = refs[:-3], refs[-3:]
    else:
        refs, (acc_out, top_out, total_out) = refs[:-3], refs[-3:]
    count = heads_step * group
    steps = refs[0].shape[1] // HEAD_DIM // heads_step
    needed = functools.reduce(jnp.maximum, places) + rows > start

    def put(j, i, total, out, top=None):
        if last:
            out = (out / total).astype(jnp.bfloat16)
        else:
            if top is not None:
                top_out[j * count + i] = top
            total_out[j * count + i] = total
        put_head(acc_out, j, count, i, out)

    def attend(j, exact):
        qs, befores = heads_of(q_ref, j, count), heads_of(acc_in, j, count)
        tiles = [heads_of(r, j, heads_step) for r in refs]
        at = lax.broadcasted_iota(jnp.int32, (rows, HEAD_DIM), 0)
        high = None
        for h in range(heads_step):
            ks, vs = choose(plane, core, [t[h] for t in tiles])
            k = jnp.concatenate(ks, axis=0)
            ok = [jnp.where(at + place >= start, 1.0, 0.0).astype(jnp.bfloat16) for place in places]
            v = jnp.concatenate([with_ones(v, o) for v, o in zip(vs, ok)], axis=0)
            members = range(h * group, (h + 1) * group)
            s_all = scores(jnp.concatenate([qs[i] for i in members], axis=0), k)
            sums, w_all = [], []
            for n, i in enumerate(members):
                s = s_all[n * rows:(n + 1) * rows]
                top, total, before = top_in[j * count + i], total_in[j * count + i], befores[i]
                if exact:
                    key = lax.broadcasted_iota(jnp.int32, (rows, rows), 1)
                    allowed = jnp.concatenate([key + place >= start for place in places], axis=1)
                    s = jnp.where(allowed, s, NEG)
                    new = jnp.maximum(top, jnp.max(s, axis=1, keepdims=True))
                    back = jnp.exp2((top - new) * SCALE)
                    top, total, before = new, total * back, before * back
                w = []
                for m in range(k.shape[0] // HEAD_DIM):
                    part = jnp.exp2((s[:, m * HEAD_DIM:(m + 1) * HEAD_DIM] - top) * SCALE).astype(jnp.bfloat16)
                    w.append(part)
                    if not exact:
                        high = part if high is None else jnp.maximum(high, part)
                w_all.append(jnp.concatenate(w, axis=1))
                sums.append((top if exact else None, total, before))
            both_all = jnp.dot(jnp.concatenate(w_all, axis=0), v, preferred_element_type=jnp.float32)
            for n, i in enumerate(members):
                both = both_all[n * rows:(n + 1) * rows]
                top, total, before = sums[n]
                put(j, i, total + both[:, HEAD_DIM:], both[:, :HEAD_DIM] + before, top)
        return high

    def step(j, _):
        @pl.when(needed)
        def _():
            high = attend(j, False)

            @pl.when(jnp.max(high.astype(jnp.float32)) > HIGH)
            def _():
                attend(j, True)

        @pl.when(jnp.logical_not(needed))
        def _():
            for i, before in enumerate(heads_of(acc_in, j, count)):
                put(j, i, total_in[j * count + i], before)

        if last:
            part(j).start()
        return 0

    def part(j):
        width = count * HEAD_DIM
        columns = pl.ds(pl.multiple_of(j * width, width), width)
        return pltpu.make_async_copy(acc_out.at[:, columns], hbm.at[:, columns], sems.at[j])

    lax.fori_loop(0, steps, step, 0)
    if last:
        for j in range(steps):
            part(j).wait()


def pick(plane, at0, at1, at2, at3):
    return jnp.where(plane == 0, at0, jnp.where(plane == 1, at1, jnp.where(plane == 2, at2, at3)))


def choose_first(plane, core, tiles):
    return tiles[:1], tiles[1:]


def devices_first(plane, core, base):
    return (jnp.where(core == 1, base, jnp.where(plane == 0, base - 7, -1)),)


def choose_middle(plane, core, tiles):
    def half(x1, y1, x2, y2, z2):
        pk, pv = pick(plane, x2, x2, y2, x2), pick(plane, z2, x1, y1, x1)
        qk, qv = pick(plane, y2, y2, x2, y2), pick(plane, z2, z2, z2, y1)
        return (pk, qk), (pv, qv)
    a, b = half(*tiles[:5]), half(*tiles[5:])
    return a[0] + b[0], a[1] + b[1]


def devices_middle(plane, core, base):
    p = base - 2 * pick(plane, 3, 1, 2, 1)
    q = pick(plane, -8, base - 4, base - 6, base - 4)
    return p + core, q + core, p + 1 - core, q + 1 - core


def choose_last(plane, core, tiles):
    z1, y2, x3, y3, z3 = tiles
    pk, pv = pick(plane, y2, x3, x3, x3), pick(plane, z3, y3, y3, y3)
    qk, qv = pick(plane, x3, z1, z1, z1), pick(plane, y3, z3, z3, z3)
    return (pk, qk), (pv, qv)


def devices_last(mates, plane, core, base):
    part = 1 - core if mates else core
    return base - 2 * pick(plane, 2, 3, 1, 3) + part, base - 2 * pick(plane, 1, 4, 4, 4) + part


def call(kernel, ids, docs, q, carry, pieces, keys, last=False):
    rows, width = q.shape
    steps = pieces[0].shape[1] // HEAD_DIM // HEADS_STEP
    group = width // pieces[0].shape[1]
    vmem = pl.BlockSpec(memory_space=pltpu.VMEM)
    arrays = [docs, q, *carry, *pieces]
    if last:
        out_shape = [jax.ShapeDtypeStruct(q.shape, jnp.bfloat16)]
        scratch = [pltpu.VMEM(q.shape, jnp.bfloat16), pltpu.SemaphoreType.DMA((steps,))]
    else:
        out_shape = [jax.ShapeDtypeStruct(q.shape, jnp.float32)]
        out_shape += [jax.ShapeDtypeStruct((width // HEAD_DIM, rows, HEAD_DIM), jnp.float32)] * 2
        scratch = []
    return pl.pallas_call(
        functools.partial(kernel, group),
        in_specs=[pl.BlockSpec(memory_space=pltpu.SMEM)] + [vmem] * len(arrays),
        out_specs=[pl.BlockSpec(memory_space=pl.ANY) if last else vmem] * len(out_shape),
        out_shape=out_shape,
        scratch_shapes=scratch,
        input_output_aliases={4: 1} if carry and not last else {},
        cost_estimate=pl.CostEstimate(
            flops=8 * rows * keys * width, bytes_accessed=4 * keys * width, transcendentals=0
        ),
        compiler_params=pltpu.CompilerParams(vmem_limit_bytes=VMEM_BYTES),
    )(ids, *arrays)


def mix_kernel(rule, ids, *refs):
    rule(ids[0] % 4, *refs)


def mix(rule, ids, arrays, count, flops=0):
    vmem = pl.BlockSpec(memory_space=pltpu.VMEM)
    return pl.pallas_call(
        functools.partial(mix_kernel, rule),
        in_specs=[pl.BlockSpec(memory_space=pltpu.SMEM)] + [vmem] * len(arrays),
        out_specs=[vmem] * count,
        out_shape=[jax.ShapeDtypeStruct(arrays[0].shape, arrays[0].dtype)] * count,
        cost_estimate=pl.CostEstimate(flops=flops, bytes_accessed=arrays[0].size, transcendentals=0),
        compiler_params=pltpu.CompilerParams(vmem_limit_bytes=VMEM_BYTES),
    )(ids, *arrays)


def mix_round2(plane, keys, z1, across, side):
    across[...] = jnp.where(plane % 2 == 0, keys[...], z1[...])
    side[...] = jnp.where(plane // 2 == 0, keys[...], z1[...])


def mix_up(plane, x1, y1, up):
    up[...] = jnp.where(plane == 1, y1[...], x1[...])


def mix_round3(plane, x1, z2, y1, values, side, up):
    side[...] = jnp.where(plane // 2 == 0, x1[...], z2[...])
    up[...] = jnp.where(plane == 0, y1[...], values[...])


def shards(queries, keys, values, doc_ids):
    rows = queries.shape[0]
    chips, cores = lax.axis_size("section"), lax.axis_size("attn")
    chip, core = lax.axis_index("section"), lax.axis_index("attn")

    def routes(target):
        return [
            (c * cores + k, at * cores + to)
            for c in range(chips) for k in range(cores) for at, to in [target(c, k)]
        ]

    along = {
        "x": routes(lambda c, k: (c ^ 1, k)),
        "y": routes(lambda c, k: (c ^ 2, k)),
        "z": routes(lambda c, k: ((c + 4) % chips, k)),
        "mate": routes(lambda c, k: (c, 1 - k)),
        "first_z": routes(lambda c, k: ((c + 4) % chips, k) if c % 4 else (c, 1 - k)),
        "first_mate": routes(lambda c, k: ((c + 4) % chips, 0) if c % 4 == 0 and k else (c, 1 - k)),
    }

    def send(array, way):
        return lax.ppermute(array, AXES, along[way])

    def swap(*arrays):
        return tuple(send(a, "mate") for a in arrays)

    ids = jnp.stack([chip, core, jnp.int32(cores)])
    docs = doc_ids.reshape(-1, HEAD_DIM)

    def far(choose, devices, carry, pieces, keys, last=False, heads_step=HEADS_STEP):
        kernel = functools.partial(far_kernel, choose, devices, last, heads_step)
        return call(kernel, ids, docs, queries, carry, pieces, keys, last)

    z1 = send(keys, "first_z")
    x1, y1 = send(values, "x"), send(values, "y")
    mate_k, mate_v = send(keys, "first_mate"), send(values, "first_mate")
    carry = call(own_kernel, ids, docs, queries, (), [keys, values], rows)
    z1, *carry = barrier((z1, *carry))
    across2, side2 = mix(mix_round2, ids, [keys, z1], 2)
    x2, y2 = send(across2, "x"), send(side2, "y")
    x1, y1, _, _ = barrier((x1, y1, across2, side2))
    (up2,) = mix(mix_up, ids, [x1, y1], 1, 2 * 10**10)
    z2 = send(up2, "z")
    carry = far(choose_first, devices_first, carry, [mate_k, mate_v], 0)
    y2, z2, y1, x1, *carry = barrier((y2, z2, y1, x1, *carry))
    x1s, y1s = swap(x1, y1)
    x3 = send(y2, "x")
    side3, up3 = mix(mix_round3, ids, [x1, z2, y1, values], 2, 2 * 10**10)
    y3, z3 = send(side3, "y"), send(up3, "z")
    x2s, y2s, z2s = swap(x2, y2, z2)
    carry = far(
        choose_middle, devices_middle, carry, [x1, y1, x2, y2, z2, x1s, y1s, x2s, y2s, z2s], 0
    )
    x3, y3, z3, *carry = barrier((x3, y3, z3, *carry))
    z1s, x3s, y3s, z3s = swap(z1, x3, y3, z3)
    carry = far(
        choose_last, functools.partial(devices_last, False), carry, [z1, y2, x3, y3, z3], 2 * rows,
        heads_step=2 * HEADS_STEP,
    )
    (out,) = far(
        choose_last, functools.partial(devices_last, True), carry, [z1s, y2s, x3s, y3s, z3s], 2 * rows, True
    )
    return out


def solution(mesh):
    split = P(AXES, None)
    return jax.shard_map(
        shards, mesh=mesh, in_specs=(split, split, split, P()), out_specs=split, check_vma=False
    )
```

```python
import functools
import math

import jax
import jax.numpy as jnp
from jax import lax
from jax.experimental import pallas as pl
from jax.experimental.pallas import tpu as pltpu
from jax.sharding import PartitionSpec as P

HEAD_DIM = 128
REACH = 8
AXES = ("section", "attn")
NEG = -1e30
SCALE = HEAD_DIM ** -0.5 * math.log2(math.e)
HEADS_STEP = 4
VMEM_BYTES = 8 * 2**20
HIGH = 2.0 ** 60
barrier = lax.optimization_barrier


def scores(q, k):
    return lax.dot_general(q, k, (((1,), (1,)), ((), ())), preferred_element_type=jnp.float32)


def heads_of(ref, step, count):
    at = pl.multiple_of(step * (count * HEAD_DIM), HEAD_DIM)
    return [ref[:, pl.ds(at + i * HEAD_DIM, HEAD_DIM)] for i in range(count)]


def put_head(ref, step, count, i, value):
    at = pl.multiple_of(step * (count * HEAD_DIM), HEAD_DIM)
    ref[:, pl.ds(at + i * HEAD_DIM, HEAD_DIM)] = value


def with_ones(v, ok):
    return jnp.concatenate([v * ok, ok], axis=1)


def where_am_i(ids, docs_ref, rows):
    chip, core = ids[0], ids[1]
    first = (chip * ids[2] + core) * rows
    head = docs_ref[pl.ds(first // HEAD_DIM, 1), :][:, :1]
    earlier = (docs_ref[...] < head).astype(jnp.int32)
    return chip, core, first, jnp.sum(earlier), head


def own_kernel(group, ids, docs_ref, q_ref, k_ref, v_ref, acc_ref, top_ref, total_ref):
    rows = q_ref.shape[0]
    count = HEADS_STEP * group
    _, _, first, _, head = where_am_i(ids, docs_ref, rows)
    tiles = [docs_ref[pl.ds(first // HEAD_DIM + i, 1), :] for i in range(rows // HEAD_DIM)]
    across = jnp.concatenate(tiles, axis=1)
    down = jnp.concatenate([jnp.broadcast_to(t, (HEAD_DIM, HEAD_DIM)).T for t in tiles], axis=0)
    same = jnp.concatenate([down] * (rows // HEAD_DIM), axis=1) == across
    at = lax.broadcasted_iota(jnp.int32, (rows, rows), 1)
    row = lax.broadcasted_iota(jnp.int32, (rows, rows), 0)
    bias = jnp.where(same & (at <= row), 0.0, NEG)
    sees_earlier = down == head

    def step(j, _):
        qs = heads_of(q_ref, j, count)
        ks, vs = heads_of(k_ref, j, HEADS_STEP), heads_of(v_ref, j, HEADS_STEP)
        for i in range(count):
            s = scores(qs[i], ks[i // group]) + bias
            top = jnp.max(s, axis=1, keepdims=True)
            w = jnp.exp2((s - top) * SCALE).astype(jnp.bfloat16)
            v = vs[i // group]
            both = jnp.dot(w, with_ones(v, jnp.ones_like(v)), preferred_element_type=jnp.float32)
            put_head(acc_ref, j, count, i, both[:, :HEAD_DIM])
            total_ref[j * count + i] = both[:, HEAD_DIM:]
            top_ref[j * count + i] = jnp.where(sees_earlier, jnp.broadcast_to(top, (rows, HEAD_DIM)), -NEG)
        return 0

    lax.fori_loop(0, k_ref.shape[1] // HEAD_DIM // HEADS_STEP, step, 0)


def far_kernel(choose, devices, last, heads_step, group, ids, docs_ref, q_ref, acc_in, top_in, total_in, *refs):
    rows = q_ref.shape[0]
    chip, core, first, start, _ = where_am_i(ids, docs_ref, rows)
    plane, owner = chip % 4, first // rows
    places = [jnp.where((d >= 0) & (d < owner), d * rows, -(2**30)) for d in devices(plane, core, chip * ids[2])]
    if last:
        refs, (hbm, acc_out, sems) = refs[:-3], refs[-3:]
    else:
        refs, (acc_out, top_out, total_out) = refs[:-3], refs[-3:]
    count = heads_step * group
    steps = refs[0].shape[1] // HEAD_DIM // heads_step
    needed = functools.reduce(jnp.maximum, places) + rows > start

    def put(j, i, total, out, top=None):
        if last:
            out = (out / total).astype(jnp.bfloat16)
        else:
            if top is not None:
                top_out[j * count + i] = top
            total_out[j * count + i] = total
        put_head(acc_out, j, count, i, out)

    def attend(j, exact):
        qs, befores = heads_of(q_ref, j, count), heads_of(acc_in, j, count)
        tiles = [heads_of(r, j, heads_step) for r in refs]
        at = lax.broadcasted_iota(jnp.int32, (rows, HEAD_DIM), 0)
        high = None
        for h in range(heads_step):
            ks, vs = choose(plane, core, [t[h] for t in tiles])
            k = jnp.concatenate(ks, axis=0)
            ok = [jnp.where(at + place >= start, 1.0, 0.0).astype(jnp.bfloat16) for place in places]
            v = jnp.concatenate([with_ones(v, o) for v, o in zip(vs, ok)], axis=0)
            members = range(h * group, (h + 1) * group)
            s_all = scores(jnp.concatenate([qs[i] for i in members], axis=0), k)
            sums, w_all = [], []
            for n, i in enumerate(members):
                s = s_all[n * rows:(n + 1) * rows]
                top, total, before = top_in[j * count + i], total_in[j * count + i], befores[i]
                if exact:
                    key = lax.broadcasted_iota(jnp.int32, (rows, rows), 1)
                    allowed = jnp.concatenate([key + place >= start for place in places], axis=1)
                    s = jnp.where(allowed, s, NEG)
                    new = jnp.maximum(top, jnp.max(s, axis=1, keepdims=True))
                    back = jnp.exp2((top - new) * SCALE)
                    top, total, before = new, total * back, before * back
                w = []
                for m in range(k.shape[0] // HEAD_DIM):
                    part = jnp.exp2((s[:, m * HEAD_DIM:(m + 1) * HEAD_DIM] - top) * SCALE).astype(jnp.bfloat16)
                    w.append(part)
                    if not exact:
                        high = part if high is None else jnp.maximum(high, part)
                w_all.append(jnp.concatenate(w, axis=1))
                sums.append((top if exact else None, total, before))
            both_all = jnp.dot(jnp.concatenate(w_all, axis=0), v, preferred_element_type=jnp.float32)
            for n, i in enumerate(members):
                both = both_all[n * rows:(n + 1) * rows]
                top, total, before = sums[n]
                put(j, i, total + both[:, HEAD_DIM:], both[:, :HEAD_DIM] + before, top)
        return high

    def step(j, _):
        @pl.when(needed)
        def _():
            high = attend(j, False)

            @pl.when(jnp.max(high.astype(jnp.float32)) > HIGH)
            def _():
                attend(j, True)

        @pl.when(jnp.logical_not(needed))
        def _():
            for i, before in enumerate(heads_of(acc_in, j, count)):
                put(j, i, total_in[j * count + i], before)

        if last:
            part(j).start()
        return 0

    def part(j):
        width = count * HEAD_DIM
        columns = pl.ds(pl.multiple_of(j * width, width), width)
        return pltpu.make_async_copy(acc_out.at[:, columns], hbm.at[:, columns], sems.at[j])

    lax.fori_loop(0, steps, step, 0)
    if last:
        for j in range(steps):
            part(j).wait()


def pick(plane, at0, at1, at2, at3):
    return jnp.where(plane == 0, at0, jnp.where(plane == 1, at1, jnp.where(plane == 2, at2, at3)))


def choose_first(plane, core, tiles):
    return tiles[:1], tiles[1:]


def devices_first(plane, core, base):
    return (jnp.where(core == 1, base, jnp.where(plane == 0, base - 7, -1)),)


def choose_middle(plane, core, tiles):
    def half(x1, y1, x2, y2, z2):
        pk, pv = pick(plane, x2, x2, y2, x2), pick(plane, z2, x1, y1, x1)
        qk, qv = pick(plane, y2, y2, x2, y2), pick(plane, z2, z2, z2, y1)
        return (pk, qk), (pv, qv)
    a, b = half(*tiles[:5]), half(*tiles[5:])
    return a[0] + b[0], a[1] + b[1]


def devices_middle(plane, core, base):
    p = base - 2 * pick(plane, 3, 1, 2, 1)
    q = pick(plane, -8, base - 4, base - 6, base - 4)
    return p + core, q + core, p + 1 - core, q + 1 - core


def choose_last(plane, core, tiles):
    z1, y2, x3, y3, z3 = tiles
    pk, pv = pick(plane, y2, x3, x3, x3), pick(plane, z3, y3, y3, y3)
    qk, qv = pick(plane, x3, z1, z1, z1), pick(plane, y3, z3, z3, z3)
    return (pk, qk), (pv, qv)


def devices_last(mates, plane, core, base):
    part = 1 - core if mates else core
    return base - 2 * pick(plane, 2, 3, 1, 3) + part, base - 2 * pick(plane, 1, 4, 4, 4) + part


def call(kernel, ids, docs, q, carry, pieces, keys, last=False):
    rows, width = q.shape
    steps = pieces[0].shape[1] // HEAD_DIM // HEADS_STEP
    group = width // pieces[0].shape[1]
    vmem = pl.BlockSpec(memory_space=pltpu.VMEM)
    arrays = [docs, q, *carry, *pieces]
    if last:
        out_shape = [jax.ShapeDtypeStruct(q.shape, jnp.bfloat16)]
        scratch = [pltpu.VMEM(q.shape, jnp.bfloat16), pltpu.SemaphoreType.DMA((steps,))]
    else:
        out_shape = [jax.ShapeDtypeStruct(q.shape, jnp.float32)]
        out_shape += [jax.ShapeDtypeStruct((width // HEAD_DIM, rows, HEAD_DIM), jnp.float32)] * 2
        scratch = []
    return pl.pallas_call(
        functools.partial(kernel, group),
        in_specs=[pl.BlockSpec(memory_space=pltpu.SMEM)] + [vmem] * len(arrays),
        out_specs=[pl.BlockSpec(memory_space=pl.ANY) if last else vmem] * len(out_shape),
        out_shape=out_shape,
        scratch_shapes=scratch,
        input_output_aliases={4: 1} if carry and not last else {},
        cost_estimate=pl.CostEstimate(
            flops=8 * rows * keys * width, bytes_accessed=4 * keys * width, transcendentals=0
        ),
        compiler_params=pltpu.CompilerParams(vmem_limit_bytes=VMEM_BYTES),
    )(ids, *arrays)


def mix_kernel(rule, ids, *refs):
    rule(ids[0] % 4, *refs)


def mix(rule, ids, arrays, count, flops=0):
    vmem = pl.BlockSpec(memory_space=pltpu.VMEM)
    return pl.pallas_call(
        functools.partial(mix_kernel, rule),
        in_specs=[pl.BlockSpec(memory_space=pltpu.SMEM)] + [vmem] * len(arrays),
        out_specs=[vmem] * count,
        out_shape=[jax.ShapeDtypeStruct(arrays[0].shape, arrays[0].dtype)] * count,
        cost_estimate=pl.CostEstimate(flops=flops, bytes_accessed=arrays[0].size, transcendentals=0),
        compiler_params=pltpu.CompilerParams(vmem_limit_bytes=VMEM_BYTES),
    )(ids, *arrays)


def mix_round2(plane, keys, z1, across, side):
    across[...] = jnp.where(plane % 2 == 0, keys[...], z1[...])
    side[...] = jnp.where(plane // 2 == 0, keys[...], z1[...])


def mix_up(plane, x1, y1, up):
    up[...] = jnp.where(plane == 1, y1[...], x1[...])


def mix_round3(plane, x1, z2, y1, values, side, up):
    side[...] = jnp.where(plane // 2 == 0, x1[...], z2[...])
    up[...] = jnp.where(plane == 0, y1[...], values[...])


def shards(queries, keys, values, doc_ids):
    rows = queries.shape[0]
    chips, cores = lax.axis_size("section"), lax.axis_size("attn")
    chip, core = lax.axis_index("section"), lax.axis_index("attn")

    def routes(target):
        return [
            (c * cores + k, at * cores + to)
            for c in range(chips) for k in range(cores) for at, to in [target(c, k)]
        ]

    along = {
        "x": routes(lambda c, k: (c ^ 1, k)),
        "y": routes(lambda c, k: (c ^ 2, k)),
        "z": routes(lambda c, k: ((c + 4) % chips, k)),
        "mate": routes(lambda c, k: (c, 1 - k)),
        "first_z": routes(lambda c, k: ((c + 4) % chips, k) if c % 4 else (c, 1 - k)),
        "first_mate": routes(lambda c, k: ((c + 4) % chips, 0) if c % 4 == 0 and k else (c, 1 - k)),
    }

    def send(array, way):
        return lax.ppermute(array, AXES, along[way])

    def swap(*arrays):
        return tuple(send(a, "mate") for a in arrays)

    ids = jnp.stack([chip, core, jnp.int32(cores)])
    docs = doc_ids.reshape(-1, HEAD_DIM)

    def far(choose, devices, carry, pieces, keys, last=False, heads_step=HEADS_STEP):
        kernel = functools.partial(far_kernel, choose, devices, last, heads_step)
        return call(kernel, ids, docs, queries, carry, pieces, keys, last)

    z1 = send(keys, "first_z")
    x1, y1 = send(values, "x"), send(values, "y")
    mate_k, mate_v = send(keys, "first_mate"), send(values, "first_mate")
    carry = call(own_kernel, ids, docs, queries, (), [keys, values], rows)
    z1, *carry = barrier((z1, *carry))
    across2, side2 = mix(mix_round2, ids, [keys, z1], 2)
    x2, y2 = send(across2, "x"), send(side2, "y")
    x1, y1, _, _ = barrier((x1, y1, across2, side2))
    (up2,) = mix(mix_up, ids, [x1, y1], 1, 2 * 10**10)
    z2 = send(up2, "z")
    carry = far(choose_first, devices_first, carry, [mate_k, mate_v], 0)
    x1, y1, *carry = barrier((x1, y1, *carry))
    x1s, y1s = swap(x1, y1)
    y2, z2, y1, x1, *carry = barrier((y2, z2, y1, x1, *carry))
    x3 = send(y2, "x")
    side3, up3 = mix(mix_round3, ids, [x1, z2, y1, values], 2, 2 * 10**10)
    y3, z3 = send(side3, "y"), send(up3, "z")
    x2s, y2s, z2s = swap(x2, y2, z2)
    carry = far(
        choose_middle, devices_middle, carry, [x1, y1, x2, y2, z2, x1s, y1s, x2s, y2s, z2s], 0
    )
    x3, y3, z3, *carry = barrier((x3, y3, z3, *carry))
    z1s, x3s, y3s, z3s = swap(z1, x3, y3, z3)
    carry = far(
        choose_last, functools.partial(devices_last, False), carry, [z1, y2, x3, y3, z3], 2 * rows,
        heads_step=2 * HEADS_STEP,
    )
    (out,) = far(
        choose_last, functools.partial(devices_last, True), carry, [z1s, y2s, x3s, y3s, z3s], 2 * rows, True
    )
    return out


def solution(mesh):
    split = P(AXES, None)
    return jax.shard_map(
        shards, mesh=mesh, in_specs=(split, split, split, P()), out_specs=split, check_vma=False
    )
```
